512 devices in a mesh: row: 16 (over y_lo, z), col: 32 (over x, y_hi, core).
Axes of the slice: x: 4, y: 8 (y_hi: 4, y_lo: 2; y = y_hi * 2 + y_lo), z: 8, core: 2. Of those that a mesh axis runs over, the one named last changes fastest.
Arguments:
- iterate: bfloat16 [3584, 18432], P('row', 'col'), as said below
Outputs:
- update: bfloat16 [3584, 18432], P('row', 'col')
Inputs may be any that keep to these rules, and one draw needn't show every extreme that they name: An iterate of the orthogonalization, with spectral norm of order one.
All inputs are finite; a program needn't handle non-finite values.
Results may differ from the reference program's by a relative error of at most 0.018.
Values may be sent and summed in bfloat16 or wider, within the bound.
A program may use at most 64 MiB of HBM per device.

```python
import math
import jax
import jax.numpy as jnp
from jax import lax

M = 3584
N = 18432
N_COL = 32


coherent_rank = 16


def shape_iterate(random_part, row_key, col_key, left_key, right_key, row_top, col_top, strength, growth):
    row_mean = math.sqrt((row_top * row_top - 1.0) / (2.0 * math.log(row_top)))
    col_mean = math.sqrt((col_top * col_top - 1.0) / (2.0 * math.log(col_top)))
    row_scale = jnp.exp(jax.random.uniform(row_key, (M, 1), jnp.float32) * math.log(row_top)) / row_mean
    col_scale = jnp.exp(jax.random.uniform(col_key, (1, N), jnp.float32) * math.log(col_top)) / col_mean
    left_factor = jax.random.normal(left_key, (M, coherent_rank), jnp.float32)
    right_factor = jax.random.normal(right_key, (coherent_rank, N), jnp.float32)
    coherent = jnp.zeros((M, N), jnp.float32)
    for index in range(coherent_rank):
        coherent = coherent + left_factor[:, index:index + 1] * right_factor[index:index + 1, :]
    edge_value = math.sqrt(N) + math.sqrt(M)
    strength_scale = strength * edge_value / math.sqrt(M * N / coherent_rank) / math.sqrt(coherent_rank)
    combined = (row_scale * random_part + strength_scale * coherent) * col_scale
    return (0.95 / (growth * edge_value) * combined).astype(jnp.bfloat16)


def draw_iterate(key, part):
    key = jax.random.fold_in(key, 11)
    noise_key, row_key, col_key, left_key, right_key = jax.random.split(key, 5)
    random_part = jax.random.truncated_normal(noise_key, -4.0, 4.0, (M, N), jnp.float32)
    return shape_iterate(random_part, row_key, col_key, left_key, right_key, 1.5, 4.0, 1.1, 1.35)


def setup_inputs(seed: int = 0) -> dict:
    key_of = jax.random.split(jax.random.key(seed), 2)
    return {
        "iterate": draw_iterate(jax.random.fold_in(key_of[1], 71), 0),
    }


coef_a = 3.4445
coef_b = -4.775
coef_c = 2.0315

def reference(iterate):
    width = N // N_COL
    blocks = iterate.reshape(M, N_COL, width).transpose(1, 0, 2)

    def add_block(total, block):
        term = jnp.dot(block, block.T, preferred_element_type=jnp.float32).astype(jnp.bfloat16)
        term = lax.optimization_barrier(term)
        return (total + term.astype(jnp.float32), None)
    summed, unused = lax.scan(add_block, jnp.zeros((M, M), jnp.float32), blocks)
    gram = summed.astype(jnp.bfloat16)
    squared = jnp.dot(gram, gram, preferred_element_type=jnp.float32)
    factor = (coef_b * gram.astype(jnp.float32) + coef_c * squared).astype(jnp.bfloat16)
    result = coef_a * iterate.astype(jnp.float32) + jnp.dot(factor, iterate, preferred_element_type=jnp.float32)
    return (math.sqrt(N) * result).astype(jnp.bfloat16)
```

```python
import math

import jax
import jax.numpy as jnp
from jax import lax
from jax.experimental import pallas as pl
from jax.experimental.pallas import tpu as pltpu
from jax.sharding import PartitionSpec as P

MESH = pl.DeviceIdType.MESH
coef_a = 3.4445
coef_b = -4.775
coef_c = 2.0315

Z, X, YH = 8, 4, 4
N_ROW = 2 * Z

X_AT = 0
CORE_AT = X_AT + 15
XR_AT = CORE_AT + 16
YR_AT = XR_AT + 16
A_AT = YR_AT + 3
B_AT = A_AT + 16
BC_AT = B_AT + 15
F_AT = BC_AT + 16
FC_AT = F_AT + 16
N_SEM = FC_AT + 16

KIND = {
    "f1": (0, -1), "f2": (0, -2), "f3": (0, -3), "f4": (0, -4),
    "b1": (0, 1), "b2": (0, 2), "b3": (0, 3),
    "o1": (1, -1), "o2": (1, -2), "o3": (1, -3),
    "y0": (1, 0), "y1": (1, 1), "y2": (1, 2), "y3": (1, 3), "y4": (1, 4),
}
NUMBER = {name: i for i, name in enumerate(KIND)}
STAGES = (
    (("f1", (("f", "f2"),)), ("b1", (("b", "b2"), ("y", "y1"))), ("y0", (("f", "o1"),))),
    (("f2", (("f", "f3"),)), ("b2", (("b", "b3"), ("y", "y2"))), ("o1", (("f", "o2"),)), ("y1", ())),
    (("f3", (("f", "f4"),)), ("b3", (("y", "y3"),)), ("o2", (("f", "o3"),)), ("y2", ())),
    (("f4", (("y", "y4"),)), ("o3", ()), ("y3", ())),
    (("y4", ()),),
)


def kernel(
    scale, x_ref, o_ref, xbuf, pbuf, cbuf, ysum, xrecv, ysend, yrecv, abuf, bbuf, fbuf, acc, send_sem, recv_sem
):
    rows, half = x_ref.shape[0], x_ref.shape[0] // 2
    r, c = lax.axis_index("row"), lax.axis_index("col")
    yl, z = r // Z, lax.rem(r, Z)
    x, yh, k = c // (2 * YH), lax.rem(c // 2, YH), lax.rem(c, 2)
    me = c // 2
    e = 1 - 2 * k
    mine = pl.ds(pl.multiple_of(k * half, half), half)
    other = pl.ds(pl.multiple_of((1 - k) * half, half), half)

    def at_row(side, steps):
        return lax.rem(yl + side, 2) * Z + lax.rem(z + steps * e + 2 * Z, Z)

    def at_col(dx, dy, dk=0):
        return lax.rem(x + dx, X) * (2 * YH) + lax.rem(yh + dy, YH) * 2 + lax.rem(k + dk, 2)

    link = {"f": (at_row(0, 1), c), "b": (at_row(0, -1), c), "y": (at_row(1, 0), c)}
    sibling = (r, at_col(0, 0, 1))

    barrier = pltpu.get_barrier_semaphore()
    partners = [*link.values(), sibling]
    partners += [(r, at_col(i, 0)) for i in range(1, X)] + [(r, at_col(0, j)) for j in range(1, YH)]
    for partner in partners:
        pl.semaphore_signal(barrier, inc=1, device_id=partner, device_id_type=MESH)
    pl.semaphore_wait(barrier, len(partners))

    def copy(src, dst, sent, received, device):
        return pltpu.make_async_remote_copy(
            src_ref=src, dst_ref=dst, send_sem=send_sem.at[sent], recv_sem=recv_sem.at[received],
            device_id=device, device_id_type=MESH,
        )

    def arrived(dst, received):
        copy(dst, dst, received, received, sibling).wait_recv()

    def left(src, sent):
        copy(src, src, sent, sent, sibling).wait_send()

    def x_send(src, at, name, s):
        number = X_AT + NUMBER[name]
        copy(src, xbuf.at[s], number, number, link[at]).start()

    for at, name in (("f", "f1"), ("b", "b1"), ("y", "y0")):
        x_send(x_ref, at, name, r)
    xbuf[r] = x_ref[...]

    def gram(s):
        product = lax.dot_general(
            x_ref[...], xbuf[s], (((1,), (1,)), ((), ())), preferred_element_type=jnp.float32
        )
        pbuf[s] = product.astype(jnp.bfloat16)
        copy(pbuf.at[s, other], cbuf.at[s], CORE_AT + s, CORE_AT + s, sibling).start()

    def reduce_x(s):
        arrived(cbuf.at[s], CORE_AT + s)
        total = pbuf[s, mine].astype(jnp.float32) + cbuf[s].astype(jnp.float32)
        ysum[s] = total.astype(jnp.bfloat16)
        to, place = s // YH, lax.rem(s, YH)
        apart = lax.rem(x - to + X, X)

        @pl.when(apart != 0)
        def _():
            copy(
                ysum.at[s], xrecv.at[apart, place], XR_AT + s, XR_AT + apart * YH + place,
                (r, to * (2 * YH) + yh * 2 + k),
            ).start()

    gram(r)
    pending = [r]
    for stage in STAGES:
        todo = []
        for name, onward in stage:
            s = at_row(*KIND[name])
            arrived(xbuf.at[s], X_AT + NUMBER[name])
            for at, new in onward:
                x_send(xbuf.at[s], at, new, s)
            todo.append(s)
        for s in pending:
            reduce_x(s)
        for s in todo:
            gram(s)
        pending = todo
    for s in pending:
        reduce_x(s)

    own = None
    for j in (1, 2, 3, 0):
        place = lax.rem(yh + j, YH)
        total = ysum[x * YH + place].astype(jnp.float32)
        for i in range(1, X):
            arrived(xrecv.at[i, place], XR_AT + i * YH + place)
            total = total + xrecv[i, place].astype(jnp.float32)
        if j:
            ysend[j - 1] = total.astype(jnp.bfloat16)
            copy(
                ysend.at[j - 1], yrecv.at[j - 1], YR_AT + j - 1, YR_AT + j - 1, (r, at_col(0, j))
            ).start()
        else:
            own = total
    for j in range(1, YH):
        arrived(yrecv.at[j - 1], YR_AT + j - 1)
        own = own + yrecv[j - 1].astype(jnp.float32)
    tile = own.astype(jnp.bfloat16)
    abuf[me] = tile
    bbuf[r, mine] = tile

    def b_send(src, at, name, s):
        number = B_AT + NUMBER[name]
        copy(src, bbuf.at[s, mine], number, number, link[at]).start()

    def b_share(s):
        copy(bbuf.at[s, mine], bbuf.at[s, mine], BC_AT + s, BC_AT + s, sibling).start()

    def a_spread(s, first):
        for i in range(1, X):
            copy(abuf.at[s], abuf.at[s], A_AT + first + i, A_AT + s, (r, at_col(i, 0))).start()

    for at, name in (("f", "f1"), ("b", "b1"), ("y", "y0")):
        b_send(bbuf.at[r, mine], at, name, r)
    for j in range(1, YH):
        copy(abuf.at[me], abuf.at[me], A_AT + j - 1, A_AT + me, (r, at_col(0, j))).start()
    a_spread(me, 2)
    b_share(r)
    for index, stage in enumerate(STAGES):
        for name, onward in stage:
            s = at_row(*KIND[name])
            arrived(bbuf.at[s, mine], B_AT + NUMBER[name])
            for at, new in onward:
                b_send(bbuf.at[s, mine], at, new, s)
            b_share(s)
        j = index + 1
        if j < YH:
            s = x * YH + lax.rem(yh + YH - j, YH)
            arrived(abuf.at[s], A_AT + s)
            a_spread(s, 2 + 3 * j)
    for i in range(1, X):
        for j in range(YH):
            s = lax.rem(x + i, X) * YH + lax.rem(yh + j, YH)
            arrived(abuf.at[s], A_AT + s)

    def wait_shared(s, _):
        arrived(bbuf.at[s, other], BC_AT + s)
        return 0

    lax.fori_loop(0, N_ROW, wait_shared, 0)

    def square(s, total):
        return total + jnp.dot(abuf[s], bbuf[s], preferred_element_type=jnp.float32)

    squared = lax.fori_loop(0, N_ROW, square, jnp.zeros((half, rows), jnp.float32))
    fbuf[me, mine] = (coef_b * tile.astype(jnp.float32) + coef_c * squared).astype(jnp.bfloat16)

    def f_share(s):
        copy(fbuf.at[s, mine], fbuf.at[s, mine], FC_AT + s, FC_AT + s, sibling).start()

    def f_spread(s, first):
        for i in range(1, X):
            copy(
                fbuf.at[s, mine], fbuf.at[s, mine], F_AT + first + i, F_AT + s, (r, at_col(i, 0))
            ).start()

    for j in range(1, YH):
        copy(fbuf.at[me, mine], fbuf.at[me, mine], F_AT + j - 1, F_AT + me, (r, at_col(0, j))).start()
    f_spread(me, 2)
    f_share(me)
    acc[...] = coef_a * x_ref[...].astype(jnp.float32)
    for j in range(1, YH):
        s = x * YH + lax.rem(yh + YH - j, YH)
        arrived(fbuf.at[s, mine], F_AT + s)
        f_spread(s, 2 + 3 * j)
        f_share(s)
    for i in range(1, X):
        for j in range(YH):
            s = lax.rem(x + i, X) * YH + lax.rem(yh + j, YH)
            arrived(fbuf.at[s, mine], F_AT + s)
            f_share(s)

    def apply(j, carry):
        s = lax.rem(me + j, N_ROW)
        arrived(fbuf.at[s, other], FC_AT + s)
        acc[...] += jnp.dot(fbuf[s], xbuf[s], preferred_element_type=jnp.float32)
        return carry

    lax.fori_loop(0, N_ROW, apply, 0)
    o_ref[...] = (scale * acc[...]).astype(o_ref.dtype)

    for number in range(15):
        left(x_ref, X_AT + number)
        left(abuf.at[0], A_AT + number)
        left(abuf.at[0], B_AT + number)
        left(abuf.at[0], F_AT + number)
    for j in range(YH - 1):
        left(ysend.at[j], YR_AT + j)

    def all_left(s, carry):
        left(cbuf.at[s], CORE_AT + s)
        left(cbuf.at[s], BC_AT + s)
        left(cbuf.at[s], FC_AT + s)

        @pl.when(s // YH != x)
        def _():
            left(ysum.at[s], XR_AT + s)

        return carry

    lax.fori_loop(0, N_ROW, all_left, 0)


def solution(mesh):
    def step(iterate):
        rows, width = iterate.shape
        half, n = rows // 2, width * mesh.shape["col"]
        bf16 = jnp.bfloat16

        def body(*refs):
            kernel(math.sqrt(n), *refs)

        return pl.pallas_call(
            body,
            out_shape=jax.ShapeDtypeStruct((rows, width), bf16),
            in_specs=[pl.BlockSpec(memory_space=pltpu.VMEM)],
            out_specs=pl.BlockSpec(memory_space=pltpu.VMEM),
            scratch_shapes=[
                pltpu.VMEM((N_ROW, rows, width), bf16),
                pltpu.VMEM((N_ROW, rows, rows), bf16),
                pltpu.VMEM((N_ROW, half, rows), bf16),
                pltpu.VMEM((N_ROW, half, rows), bf16),
                pltpu.VMEM((X, YH, half, rows), bf16),
                pltpu.VMEM((YH - 1, half, rows), bf16),
                pltpu.VMEM((YH - 1, half, rows), bf16),
                pltpu.VMEM((N_ROW, half, rows), bf16),
                pltpu.VMEM((N_ROW, rows, rows), bf16),
                pltpu.VMEM((N_ROW, rows, rows), bf16),
                pltpu.VMEM((rows, width), jnp.float32),
                pltpu.SemaphoreType.DMA((N_SEM,)),
                pltpu.SemaphoreType.DMA((N_SEM,)),
            ],
            compiler_params=pltpu.CompilerParams(
                collective_id=0, has_side_effects=True, vmem_limit_bytes=48 << 20
            ),
            cost_estimate=pl.CostEstimate(
                flops=2 * rows * N_ROW * rows * (2 * width + half), bytes_accessed=4 * rows * width, transcendentals=0
            ),
        )(iterate)

    return jax.shard_map(
        step, mesh=mesh, in_specs=(P("row", "col"),), out_specs=P("row", "col"), check_vma=False
    )
```

```python
import math

import jax
import jax.numpy as jnp
from jax import lax
from jax.experimental import pallas as pl
from jax.experimental.pallas import tpu as pltpu
from jax.sharding import PartitionSpec as P

MESH = pl.DeviceIdType.MESH
coef_a = 3.4445
coef_b = -4.775
coef_c = 2.0315

Z, X, YH = 8, 4, 4
N_ROW = 2 * Z

X_AT = 0
CORE_AT = X_AT + 15
XR_AT = CORE_AT + 16
D_AT = XR_AT + 16
A_AT = D_AT + 4
B_AT = A_AT + 16
BC_AT = B_AT + 15
F_AT = BC_AT + 16
FC_AT = F_AT + 16
N_SEM = FC_AT + 16

HERE = (0, 0)
KIND = {
    "m1": (0, -1), "m2": (0, -2), "m3": (0, -3), "p1": (0, 1), "p2": (0, 2), "p3": (0, 3), "q4": (0, 4),
    "y0": (1, 0), "y1": (1, 1), "y2": (1, 2), "y3": (1, 3), "r4": (1, 4), "n1": (1, -1), "n2": (1, -2), "n3": (1, -3),
}
NUMBER = {name: i for i, name in enumerate(KIND)}
ONWARD = {
    "m1": (("u", "m2"),), "m2": (("u", "m3"),), "m3": (("y", "n3"),),
    "p1": (("d", "p2"), ("y", "y1")), "p2": (("d", "p3"), ("y", "y2")), "p3": (("d", "q4"), ("y", "y3")),
    "y0": (("u", "n1"),), "n1": (("u", "n2"),), "y3": (("d", "r4"),),
}
STAGES = (("m1", "p1", "y0"), ("m2", "p2", "y1", "n1"), ("m3", "p3", "y2", "n2"), ("q4", "y3", "n3"), ("r4",))
T1, T2 = (1, 1), (1, 2)
BLOCKS = (
    (HERE, HERE), ((0, 1), (0, -1)), ((0, -1), (0, 2)), ((0, -2), T2),
    (HERE, (0, 1)), (HERE, (1, 0)), ((0, 2), (0, -1)), (HERE, T1),
    ((0, 1), HERE), ((0, -2), (0, 2)), (T1, HERE), ((0, -1), T1),
    ((0, -1), (0, 1)), (T1, (0, -1)), ((0, -2), T1), (T1, (0, -2)),
)
FIRST = (0, 4, 8, 12, 1, 5)
SECOND = (2, 6, 9, 7, 10, 11, 13, 14, 15)
LAST = (3,)


def pick(index, values):
    n = len(values)
    return sum(((n - lax.rem(index - i + n, n)) // n) * value for i, value in enumerate(values) if value)


def kernel(
    scale, x_ref, o_ref, xbuf, pbuf, cbuf, xsum, xrecv, dsend, drecv, abuf, bbuf, fbuf, acc, send_sem, recv_sem
):
    rows, half = x_ref.shape[0], x_ref.shape[0] // 2
    r, c = lax.axis_index("row"), lax.axis_index("col")
    yl, z = r // Z, lax.rem(r, Z)
    x, yh, k = c // (2 * YH), lax.rem(c // 2, YH), lax.rem(c, 2)
    me = c // 2
    mine = pl.ds(pl.multiple_of(k * half, half), half)
    other = pl.ds(pl.multiple_of((1 - k) * half, half), half)

    def at_row(side, steps):
        return lax.rem(yl + side, 2) * Z + lax.rem(z + steps + Z, Z)

    def at_col(dx, dy, dk=0):
        return lax.rem(x + dx, X) * (2 * YH) + lax.rem(yh + dy, YH) * 2 + lax.rem(k + dk, 2)

    link = {"u": (at_row(0, 1), c), "d": (at_row(0, -1), c), "y": (at_row(1, 0), c)}
    sibling = (r, at_col(0, 0, 1))

    owner, at_home = [], []
    for place in range(YH):
        column = [BLOCKS[i * YH + place] for i in range(X)]
        to_row = at_row(pick(x, [a[0] for a, b in column]), pick(x, [a[1] for a, b in column]))
        to = at_row(pick(x, [b[0] for a, b in column]), pick(x, [b[1] for a, b in column]))
        owner.append((to_row, to * 2 + k))
        at_home.append(jnp.logical_and(to_row == r, to == me))
    apart = {((b[0] - a[0]) % 2, (b[1] - a[1]) % Z): (n, a) for n, (a, b) in enumerate(BLOCKS)}
    found = [apart[side, steps] for side in range(2) for steps in range(Z)]
    from_me = lax.rem(me // Z - yl + 2, 2) * Z + lax.rem(lax.rem(me, Z) - z + Z, Z)
    from_x = pick(from_me, [n // YH for n, a in found])
    from_row = at_row(pick(from_me, [a[0] for n, a in found]), 0 - pick(from_me, [a[1] for n, a in found]))
    from_home = jnp.logical_and(from_row == r, from_x == x)

    barrier = pltpu.get_barrier_semaphore()
    partners = [*link.values(), sibling]
    partners += [(r, at_col(i, 0)) for i in range(1, X)] + [(r, at_col(0, j)) for j in range(1, YH)]
    for partner in partners:
        pl.semaphore_signal(barrier, inc=1, device_id=partner, device_id_type=MESH)
    for j in range(YH):
        there = lax.rem(yh + j, YH)

        def greet():
            pl.semaphore_signal(
                barrier, inc=1, device_id=(from_row, from_x * (2 * YH) + there * 2 + k), device_id_type=MESH
            )

        if j:
            greet()
        else:
            pl.when(jnp.logical_not(from_home))(greet)
    pl.semaphore_wait(barrier, len(partners) + YH - from_home.astype(jnp.int32))

    def copy(src, dst, sent, received, device):
        return pltpu.make_async_remote_copy(
            src_ref=src, dst_ref=dst, send_sem=send_sem.at[sent], recv_sem=recv_sem.at[received],
            device_id=device, device_id_type=MESH,
        )

    def arrived(dst, received):
        copy(dst, dst, received, received, sibling).wait_recv()

    def left(src, sent):
        copy(src, src, sent, sent, sibling).wait_send()

    def x_send(src, at, name, s):
        number = X_AT + NUMBER[name]
        copy(src, xbuf.at[s], number, number, link[at]).start()

    def x_wait(name):
        s = at_row(*KIND[name])
        arrived(xbuf.at[s], X_AT + NUMBER[name])

    def x_onward(name):
        s = at_row(*KIND[name])
        for at, new in ONWARD.get(name, ()):
            x_send(xbuf.at[s], at, new, s)

    def x_pass(*names):
        for name in names:
            x_wait(name)
            x_onward(name)

    for at, name in (("u", "m1"), ("d", "p1"), ("y", "y0")):
        x_send(x_ref, at, name, r)
    xbuf[r] = x_ref[...]

    def gram(n):
        a, b = BLOCKS[n]
        product = lax.dot_general(
            xbuf[at_row(*a)], xbuf[at_row(*b)], (((1,), (1,)), ((), ())), preferred_element_type=jnp.float32
        )
        pbuf[n] = product.astype(jnp.bfloat16)
        copy(pbuf.at[n, other], cbuf.at[n], CORE_AT + n, CORE_AT + n, sibling).start()

    def reduce_x(n):
        arrived(cbuf.at[n], CORE_AT + n)
        total = pbuf[n, mine].astype(jnp.float32) + cbuf[n].astype(jnp.float32)
        xsum[n] = total.astype(jnp.bfloat16)
        to, place = n // YH, n % YH
        apart = lax.rem(x - to + X, X)

        @pl.when(apart != 0)
        def _():
            copy(
                xsum.at[n], xrecv.at[apart, place], XR_AT + n, XR_AT + apart * YH + place,
                (r, to * (2 * YH) + yh * 2 + k),
            ).start()

    def deliver(place):
        total = xsum[x * YH + place].astype(jnp.float32)
        for i in range(1, X):
            arrived(xrecv.at[i, place], XR_AT + i * YH + place)
            total = total + xrecv[i, place].astype(jnp.float32)
        dsend[place] = total.astype(jnp.bfloat16)

        @pl.when(jnp.logical_not(at_home[place]))
        def _():
            copy(dsend.at[place], drecv.at[yh], D_AT + place, D_AT + yh, owner[place]).start()

        @pl.when(at_home[place])
        def _():
            drecv[yh] = dsend[place]

    gram(FIRST[0])
    x_wait("m1")
    x_onward("m1")
    x_wait("p1")
    x_onward("p1")
    x_wait("y0")
    for n in FIRST[1:]:
        gram(n)
    for n in FIRST:
        reduce_x(n)
    x_pass("m2", "p2")
    x_onward("y0")
    x_wait("y1")
    for n in SECOND:
        gram(n)
    for n in SECOND:
        reduce_x(n)
    x_wait("y2")
    for n in LAST:
        gram(n)
    x_pass("p3")
    for n in LAST:
        reduce_x(n)
    for place in range(YH):
        deliver(place)
    x_pass("m3", "n1")

    @pl.when(jnp.logical_not(from_home))
    def _():
        arrived(drecv.at[yh], D_AT + yh)

    own = drecv[yh].astype(jnp.float32)
    for j in range(1, YH):
        there = lax.rem(yh + j, YH)
        arrived(drecv.at[there], D_AT + there)
        own = own + drecv[there].astype(jnp.float32)
    tile = own.astype(jnp.bfloat16)
    abuf[me] = tile
    bbuf[r, mine] = tile

    def b_send(src, at, name, s):
        number = B_AT + NUMBER[name]
        copy(src, bbuf.at[s, mine], number, number, link[at]).start()

    def b_share(s):
        copy(bbuf.at[s, mine], bbuf.at[s, mine], BC_AT + s, BC_AT + s, sibling).start()

    def a_spread(s, first):
        for i in range(1, X):
            copy(abuf.at[s], abuf.at[s], A_AT + first + i, A_AT + s, (r, at_col(i, 0))).start()

    for at, name in (("u", "m1"), ("d", "p1"), ("y", "y0")):
        b_send(bbuf.at[r, mine], at, name, r)
    for j in range(1, YH):
        copy(abuf.at[me], abuf.at[me], A_AT + j - 1, A_AT + me, (r, at_col(0, j))).start()
    a_spread(me, 2)
    b_share(r)
    x_pass("y3")
    for index, stage in enumerate(STAGES):
        for name in stage:
            s = at_row(*KIND[name])
            arrived(bbuf.at[s, mine], B_AT + NUMBER[name])
            for at, new in ONWARD.get(name, ()):
                b_send(bbuf.at[s, mine], at, new, s)
            b_share(s)
        j = index + 1
        if j < YH:
            s = x * YH + lax.rem(yh + YH - j, YH)
            arrived(abuf.at[s], A_AT + s)
            a_spread(s, 2 + 3 * j)
    for i in range(1, X):
        for j in range(YH):
            s = lax.rem(x + i, X) * YH + lax.rem(yh + j, YH)
            arrived(abuf.at[s], A_AT + s)

    def wait_shared(s, _):
        arrived(bbuf.at[s, other], BC_AT + s)
        return 0

    lax.fori_loop(0, N_ROW, wait_shared, 0)

    def square(s, total):
        return total + jnp.dot(abuf[s], bbuf[s], preferred_element_type=jnp.float32)

    squared = lax.fori_loop(0, N_ROW, square, jnp.zeros((half, rows), jnp.float32))
    fbuf[me, mine] = (coef_b * tile.astype(jnp.float32) + coef_c * squared).astype(jnp.bfloat16)

    def f_share(s):
        copy(fbuf.at[s, mine], fbuf.at[s, mine], FC_AT + s, FC_AT + s, sibling).start()

    def f_spread(s, first):
        for i in range(1, X):
            copy(
                fbuf.at[s, mine], fbuf.at[s, mine], F_AT + first + i, F_AT + s, (r, at_col(i, 0))
            ).start()

    for j in range(1, YH):
        copy(fbuf.at[me, mine], fbuf.at[me, mine], F_AT + j - 1, F_AT + me, (r, at_col(0, j))).start()
    f_spread(me, 2)
    f_share(me)
    acc[...] = coef_a * x_ref[...].astype(jnp.float32)
    for j in range(1, YH):
        s = x * YH + lax.rem(yh + YH - j, YH)
        arrived(fbuf.at[s, mine], F_AT + s)
        f_spread(s, 2 + 3 * j)
        f_share(s)
    for i in range(1, X):
        for j in range(YH):
            s = lax.rem(x + i, X) * YH + lax.rem(yh + j, YH)
            arrived(fbuf.at[s, mine], F_AT + s)
            f_share(s)

    for name in ("q4", "n2", "n3", "r4"):
        x_wait(name)

    def apply(j, carry):
        s = lax.rem(me + j, N_ROW)
        arrived(fbuf.at[s, other], FC_AT + s)
        acc[...] += jnp.dot(fbuf[s], xbuf[s], preferred_element_type=jnp.float32)
        return carry

    lax.fori_loop(0, N_ROW, apply, 0)
    o_ref[...] = (scale * acc[...]).astype(o_ref.dtype)

    for number in range(15):
        left(x_ref, X_AT + number)
        left(abuf.at[0], A_AT + number)
        left(abuf.at[0], B_AT + number)
        left(abuf.at[0], F_AT + number)
    for place in range(YH):

        @pl.when(jnp.logical_not(at_home[place]))
        def _():
            left(dsend.at[place], D_AT + place)


    def all_left(s, carry):
        left(cbuf.at[s], CORE_AT + s)
        left(cbuf.at[s], BC_AT + s)
        left(cbuf.at[s], FC_AT + s)

        @pl.when(s // YH != x)
        def _():
            left(xsum.at[s], XR_AT + s)

        return carry

    lax.fori_loop(0, N_ROW, all_left, 0)


def solution(mesh):
    def step(iterate):
        rows, width = iterate.shape
        half, n = rows // 2, width * mesh.shape["col"]
        bf16 = jnp.bfloat16

        def body(*refs):
            kernel(math.sqrt(n), *refs)

        return pl.pallas_call(
            body,
            out_shape=jax.ShapeDtypeStruct((rows, width), bf16),
            in_specs=[pl.BlockSpec(memory_space=pltpu.VMEM)],
            out_specs=pl.BlockSpec(memory_space=pltpu.VMEM),
            scratch_shapes=[
                pltpu.VMEM((N_ROW, rows, width), bf16),
                pltpu.VMEM((N_ROW, rows, rows), bf16),
                pltpu.VMEM((N_ROW, half, rows), bf16),
                pltpu.VMEM((N_ROW, half, rows), bf16),
                pltpu.VMEM((X, YH, half, rows), bf16),
                pltpu.VMEM((YH, half, rows), bf16),
                pltpu.VMEM((YH, half, rows), bf16),
                pltpu.VMEM((N_ROW, half, rows), bf16),
                pltpu.VMEM((N_ROW, rows, rows), bf16),
                pltpu.VMEM((N_ROW, rows, rows), bf16),
                pltpu.VMEM((rows, width), jnp.float32),
                pltpu.SemaphoreType.DMA((N_SEM,)),
                pltpu.SemaphoreType.DMA((N_SEM,)),
            ],
            compiler_params=pltpu.CompilerParams(
                collective_id=0, has_side_effects=True, vmem_limit_bytes=48 << 20
            ),
            cost_estimate=pl.CostEstimate(
                flops=2 * rows * N_ROW * rows * (2 * width + half), bytes_accessed=4 * rows * width, transcendentals=0
            ),
        )(iterate)

    return jax.shard_map(
        step, mesh=mesh, in_specs=(P("row", "col"),), out_specs=P("row", "col"), check_vma=False
    )
```

```python
import math

import jax
import jax.numpy as jnp
from jax import lax
from jax.experimental import pallas as pl
from jax.experimental.pallas import tpu as pltpu
from jax.sharding import PartitionSpec as P

MESH = pl.DeviceIdType.MESH
coef_a = 3.4445
coef_b = -4.775
coef_c = 2.0315

Z, X, YH = 8, 4, 4
N_ROW = 2 * Z

X_AT = 0
CORE_AT = X_AT + 15
XR_AT = CORE_AT + 16
Y_AT = XR_AT + 16
G_AT = Y_AT + 4
A_AT = G_AT + 1
B_AT = A_AT + 16
BC_AT = B_AT + 15
F_AT = BC_AT + 16
FC_AT = F_AT + 16
N_SEM = FC_AT + 16

HERE = (0, 0)
KIND = {
    "m1": (0, -1), "m2": (0, -2), "m3": (0, -3), "p1": (0, 1), "p2": (0, 2), "p3": (0, 3), "q4": (0, 4),
    "y0": (1, 0), "y1": (1, 1), "y2": (1, 2), "y3": (1, 3), "r4": (1, 4), "n1": (1, -1), "n2": (1, -2), "n3": (1, -3),
}
NUMBER = {name: i for i, name in enumerate(KIND)}
ONWARD = {
    "m1": (("u", "m2"),), "m2": (("u", "m3"),), "m3": (("y", "n3"),),
    "p1": (("d", "p2"), ("y", "y1")), "p2": (("d", "p3"), ("y", "y2")), "p3": (("d", "q4"), ("y", "y3")),
    "y0": (("u", "n1"),), "n1": (("u", "n2"),), "y3": (("d", "r4"),),
}
PANEL = {
    "m1": (("y", 0, "n1"),), "p1": (("y", 0, "y1"),),
    "m2": (("z", 1, "m3"), ("y", 0, "n2")), "p2": (("z", -1, "p3"), ("z", -2, "q4"), ("y", 0, "y2")),
    "m3": (("y", 0, "n3"),), "p3": (("y", 0, "y3"),), "q4": (("y", 0, "r4"),),
}
T0, T1, T2 = (1, 0), (1, 1), (1, 2)
BLOCKS = (
    (HERE, HERE), ((0, -1), (0, 2)), ((0, 1), (0, -1)), (T1, (0, -1)),
    (HERE, (0, 1)), ((0, 2), (0, -1)), (T0, HERE), ((0, -2), T1),
    (HERE, (0, -1)), ((0, -2), (0, 2)), ((0, -1), T0), (T1, (0, -2)),
    ((0, -1), (0, 1)), ((0, -1), T1), ((0, 1), T0), ((0, -2), T2),
)
FIRST = (0, 2, 4, 6, 8, 10, 12, 14)
SECOND = (1, 3, 5, 7, 9, 11, 13)
LAST = (15,)


def pick(index, values):
    n = len(values)
    return sum(((n - lax.rem(index - i + n, n)) // n) * value for i, value in enumerate(values) if value)


def kernel(
    scale, x_ref, o_ref, xbuf, pbuf, cbuf, xsum, xrecv, ysend, yrecv, gsend, gtile, abuf, bbuf, fbuf, acc, send_sem, recv_sem
):
    rows, half = x_ref.shape[0], x_ref.shape[0] // 2
    r, c = lax.axis_index("row"), lax.axis_index("col")
    yl, z = r // Z, lax.rem(r, Z)
    x, yh, k = c // (2 * YH), lax.rem(c // 2, YH), lax.rem(c, 2)
    me = yh * X + x
    mine = pl.ds(pl.multiple_of(k * half, half), half)
    other = pl.ds(pl.multiple_of((1 - k) * half, half), half)

    def at_row(side, steps):
        return lax.rem(yl + side, 2) * Z + lax.rem(z + steps + Z, Z)

    def at_col(dx, dy, dk=0):
        return lax.rem(x + dx, X) * (2 * YH) + lax.rem(yh + dy, YH) * 2 + lax.rem(k + dk, 2)

    link = {"u": (at_row(0, 1), c), "d": (at_row(0, -1), c), "y": (at_row(1, 0), c)}
    sibling = (r, at_col(0, 0, 1))

    def block_at(number):
        return at_row(pick(number, [a[0] for a, b in BLOCKS]), pick(number, [a[1] for a, b in BLOCKS])), at_row(
            pick(number, [b[0] for a, b in BLOCKS]), pick(number, [b[1] for a, b in BLOCKS])
        )

    def column(s):
        return lax.rem(s, X) * (2 * YH) + s // X * 2 + k

    to_row, to = block_at(x * YH + yh)
    owner = (to_row, column(to))
    apart = {((b[0] - a[0]) % 2, (b[1] - a[1]) % Z): (n, a) for n, (a, b) in enumerate(BLOCKS)}
    found = [apart[side, steps] for side in range(2) for steps in range(Z)]
    from_me = lax.rem(me // Z - yl + 2, 2) * Z + lax.rem(lax.rem(me, Z) - z + Z, Z)
    from_row = at_row(pick(from_me, [a[0] for n, a in found]), 0 - pick(from_me, [a[1] for n, a in found]))
    source = (from_row, pick(from_me, [n for n, a in found]) * 2 + k)
    at_home = jnp.logical_and(to_row == r, to == me)

    barrier = pltpu.get_barrier_semaphore()
    partners = [*link.values(), sibling]
    partners += [(r, at_col(i, 0)) for i in range(1, X)] + [(r, at_col(0, j)) for j in range(1, YH)]
    for partner in partners:
        pl.semaphore_signal(barrier, inc=1, device_id=partner, device_id_type=MESH)

    @pl.when(jnp.logical_not(at_home))
    def _():
        pl.semaphore_signal(barrier, inc=1, device_id=source, device_id_type=MESH)

    pl.semaphore_wait(barrier, len(partners) + 1 - at_home.astype(jnp.int32))

    def copy(src, dst, sent, received, device):
        return pltpu.make_async_remote_copy(
            src_ref=src, dst_ref=dst, send_sem=send_sem.at[sent], recv_sem=recv_sem.at[received],
            device_id=device, device_id_type=MESH,
        )

    def arrived(dst, received):
        copy(dst, dst, received, received, sibling).wait_recv()

    def left(src, sent):
        copy(src, src, sent, sent, sibling).wait_send()

    def x_send(src, at, name, s):
        number = X_AT + NUMBER[name]
        copy(src, xbuf.at[s], number, number, link[at]).start()

    def x_wait(name):
        s = at_row(*KIND[name])
        arrived(xbuf.at[s], X_AT + NUMBER[name])

    def x_onward(name):
        s = at_row(*KIND[name])
        for at, new in ONWARD.get(name, ()):
            x_send(xbuf.at[s], at, new, s)

    def x_pass(*names):
        for name in names:
            x_wait(name)
            x_onward(name)

    for at, name in (("u", "m1"), ("d", "p1"), ("y", "y0")):
        x_send(x_ref, at, name, r)
    xbuf[r] = x_ref[...]

    def gram(n):
        a, b = BLOCKS[n]
        product = lax.dot_general(
            xbuf[at_row(*a)], xbuf[at_row(*b)], (((1,), (1,)), ((), ())), preferred_element_type=jnp.float32
        )
        pbuf[n] = product.astype(jnp.bfloat16)
        copy(pbuf.at[n, other], cbuf.at[n], CORE_AT + n, CORE_AT + n, sibling).start()

    def reduce_x(n):
        arrived(cbuf.at[n], CORE_AT + n)
        total = pbuf[n, mine].astype(jnp.float32) + cbuf[n].astype(jnp.float32)
        xsum[n] = total.astype(jnp.bfloat16)
        to, place = n // YH, n % YH
        apart = lax.rem(x - to + X, X)

        @pl.when(apart != 0)
        def _():
            copy(
                xsum.at[n], xrecv.at[apart, place], XR_AT + n, XR_AT + apart * YH + place,
                (r, to * (2 * YH) + yh * 2 + k),
            ).start()

    def reduce_y(place):
        total = xsum[x * YH + place].astype(jnp.float32)
        for i in range(1, X):
            arrived(xrecv.at[i, place], XR_AT + i * YH + place)
            total = total + xrecv[i, place].astype(jnp.float32)
        ysend[place] = total.astype(jnp.bfloat16)
        apart = lax.rem(yh - place + YH, YH)

        @pl.when(apart != 0)
        def _():
            copy(
                ysend.at[place], yrecv.at[apart], Y_AT + place, Y_AT + apart,
                (r, x * (2 * YH) + place * 2 + k),
            ).start()

    def deliver():
        total = ysend[yh].astype(jnp.float32)
        for j in range(1, YH):
            arrived(yrecv.at[j], Y_AT + j)
            total = total + yrecv[j].astype(jnp.float32)
        gsend[...] = total.astype(jnp.bfloat16)

        @pl.when(jnp.logical_not(at_home))
        def _():
            copy(gsend, gtile, G_AT, G_AT, owner).start()

        @pl.when(at_home)
        def _():
            gtile[...] = gsend[...]

    gram(FIRST[0])
    x_wait("m1")
    x_onward("m1")
    x_wait("p1")
    x_onward("p1")
    x_wait("y0")
    for n in FIRST[1:]:
        gram(n)
    for n in FIRST:
        reduce_x(n)
    x_pass("m2", "p2")
    x_onward("y0")
    x_wait("y1")
    for n in SECOND:
        gram(n)
    for place in (0, 2):
        reduce_y(place)
    for n in SECOND:
        reduce_x(n)

    @pl.when(lax.rem(yh, 2) == 0)
    def _():
        deliver()

    x_wait("y2")
    for n in LAST:
        gram(n)
    x_pass("p3")
    for n in LAST:
        reduce_x(n)
    for place in (1, 3):
        reduce_y(place)
    x_pass("m3", "n1")

    @pl.when(lax.rem(yh, 2) == 1)
    def _():
        deliver()

    @pl.when(jnp.logical_not(at_home))
    def _():
        arrived(gtile, G_AT)

    tile = gtile[...]
    abuf[me] = tile
    bbuf[r, mine] = tile

    def b_send(at, steps, name, s):
        number = B_AT + NUMBER[name]
        device = link["y"] if at == "y" else (at_row(0, steps), c)
        copy(bbuf.at[s, mine], bbuf.at[s, mine], number, number, device).start()

    def b_share(s):
        copy(bbuf.at[s, mine], bbuf.at[s, mine], BC_AT + s, BC_AT + s, sibling).start()

    def b_pass(*names):
        for name in names:
            s = at_row(*KIND[name])
            arrived(bbuf.at[s, mine], B_AT + NUMBER[name])
            b_share(s)
            for at, steps, new in PANEL.get(name, ()):
                b_send(at, steps, new, s)

    def beside(dx, dy):
        return lax.rem(yh + dy, YH) * X + lax.rem(x + dx, X)

    def a_spread(s, first):
        for i, dx in enumerate((1, 3, 2)):
            copy(abuf.at[s], abuf.at[s], A_AT + first + i, A_AT + s, (r, at_col(dx, 0))).start()

    def a_pass(number, dy):
        s = beside(0, YH - dy)
        arrived(abuf.at[s], A_AT + s)
        a_spread(s, 3 + 3 * number)

    for at, steps, name in (("z", 2, "m2"), ("z", -2, "p2"), ("z", 1, "m1"), ("z", -1, "p1"), ("y", 0, "y0")):
        b_send(at, steps, name, r)
    for j, dy in enumerate((1, 3, 2)):
        copy(abuf.at[me], abuf.at[me], A_AT + j, A_AT + me, (r, at_col(0, dy))).start()
    a_spread(me, 3)
    b_share(r)
    x_pass("y3")
    b_pass("m1", "p1", "m2", "p2")
    a_pass(1, 1)
    a_pass(2, 3)
    a_pass(3, 2)
    b_pass("m3", "p3", "q4", "y0", "n1", "y1", "n2", "y2", "n3", "y3", "r4")
    for dx in (1, 3, 2):
        for dy in range(YH):
            s = beside(dx, dy)
            arrived(abuf.at[s], A_AT + s)

    squared = jnp.zeros((half, rows), jnp.float32)
    for s in range(N_ROW):
        arrived(bbuf.at[s, other], BC_AT + s)
        squared = squared + jnp.dot(abuf[s], bbuf[s], preferred_element_type=jnp.float32)
    fbuf[me, mine] = (coef_b * tile.astype(jnp.float32) + coef_c * squared).astype(jnp.bfloat16)

    def f_share(s):
        copy(fbuf.at[s, mine], fbuf.at[s, mine], FC_AT + s, FC_AT + s, sibling).start()

    def f_spread(s, first):
        for i, dx in enumerate((1, 3, 2)):
            copy(
                fbuf.at[s, mine], fbuf.at[s, mine], F_AT + first + i, F_AT + s, (r, at_col(dx, 0))
            ).start()

    def f_apply(dx):
        for dy in range(YH):
            s = beside(dx, dy)
            arrived(fbuf.at[s, other], FC_AT + s)
            acc[...] += jnp.dot(fbuf[s], xbuf[s], preferred_element_type=jnp.float32)

    for j, dy in enumerate((1, 3, 2)):
        copy(fbuf.at[me, mine], fbuf.at[me, mine], F_AT + j, F_AT + me, (r, at_col(0, dy))).start()
    f_spread(me, 3)
    f_share(me)
    acc[...] = coef_a * x_ref[...].astype(jnp.float32)
    for name in ("q4", "n2", "n3", "r4"):
        x_wait(name)
    for j, dy in enumerate((1, 3, 2)):
        s = beside(0, YH - dy)
        arrived(fbuf.at[s, mine], F_AT + s)
        f_share(s)
        f_spread(s, 6 + 3 * j)
    done = 0
    for dx in (1, 3, 2):
        for dy in range(YH):
            s = beside(dx, dy)
            arrived(fbuf.at[s, mine], F_AT + s)
            f_share(s)
        f_apply(done)
        done = dx
    f_apply(done)
    o_ref[...] = (scale * acc[...]).astype(o_ref.dtype)

    for number in range(15):
        left(x_ref, X_AT + number)
        left(abuf.at[0], A_AT + number)
        left(abuf.at[0], B_AT + number)
        left(abuf.at[0], F_AT + number)
    for place in range(YH):

        @pl.when(yh != place)
        def _():
            left(ysend.at[place], Y_AT + place)

    @pl.when(jnp.logical_not(at_home))
    def _():
        left(gsend, G_AT)

    def all_left(s, carry):
        left(cbuf.at[s], CORE_AT + s)
        left(cbuf.at[s], BC_AT + s)
        left(cbuf.at[s], FC_AT + s)

        @pl.when(s // YH != x)
        def _():
            left(xsum.at[s], XR_AT + s)

        return carry

    lax.fori_loop(0, N_ROW, all_left, 0)


def solution(mesh):
    def step(iterate):
        rows, width = iterate.shape
        half, n = rows // 2, width * mesh.shape["col"]
        bf16 = jnp.bfloat16

        def body(*refs):
            kernel(math.sqrt(n), *refs)

        return pl.pallas_call(
            body,
            out_shape=jax.ShapeDtypeStruct((rows, width), bf16),
            in_specs=[pl.BlockSpec(memory_space=pltpu.VMEM)],
            out_specs=pl.BlockSpec(memory_space=pltpu.VMEM),
            scratch_shapes=[
                pltpu.VMEM((N_ROW, rows, width), bf16),
                pltpu.VMEM((N_ROW, rows, rows), bf16),
                pltpu.VMEM((N_ROW, half, rows), bf16),
                pltpu.VMEM((N_ROW, half, rows), bf16),
                pltpu.VMEM((X, YH, half, rows), bf16),
                pltpu.VMEM((YH, half, rows), bf16),
                pltpu.VMEM((YH, half, rows), bf16),
                pltpu.VMEM((half, rows), bf16),
                pltpu.VMEM((half, rows), bf16),
                pltpu.VMEM((N_ROW, half, rows), bf16),
                pltpu.VMEM((N_ROW, rows, rows), bf16),
                pltpu.VMEM((N_ROW, rows, rows), bf16),
                pltpu.VMEM((rows, width), jnp.float32),
                pltpu.SemaphoreType.DMA((N_SEM,)),
                pltpu.SemaphoreType.DMA((N_SEM,)),
            ],
            compiler_params=pltpu.CompilerParams(
                collective_id=0, has_side_effects=True, vmem_limit_bytes=48 << 20
            ),
            cost_estimate=pl.CostEstimate(
                flops=2 * rows * N_ROW * rows * (2 * width + half), bytes_accessed=4 * rows * width, transcendentals=0
            ),
        )(iterate)

    return jax.shard_map(
        step, mesh=mesh, in_specs=(P("row", "col"),), out_specs=P("row", "col"), check_vma=False
    )
```

```python
import functools
import math

import jax
import jax.numpy as jnp
from jax import lax
from jax.experimental import pallas as pl
from jax.experimental.pallas import tpu as pltpu
from jax.sharding import PartitionSpec as P

MESH = pl.DeviceIdType.MESH
coef_a = 3.4445
coef_b = -4.775
coef_c = 2.0315

Z, X, YH = 8, 4, 4
N_ROW = 2 * Z

X_AT = 0
CORE_AT = X_AT + 16
XR_AT = CORE_AT + 16
Y_AT = XR_AT + 16
G_AT = Y_AT + 4
A_AT = G_AT + 1
B_AT = A_AT + 16
BC_AT = B_AT + 15
F_AT = BC_AT + 16
FC_AT = F_AT + 16
N_SEM = FC_AT + 16

HERE = (0, 0)
KIND = {
    "m1": (0, -1), "m2": (0, -2), "m3": (0, -3), "p1": (0, 1), "p2": (0, 2), "p3": (0, 3), "q4": (0, 4),
    "y0": (1, 0), "y1": (1, 1), "y2": (1, 2), "y3": (1, 3), "r4": (1, 4), "n1": (1, -1), "n2": (1, -2), "n3": (1, -3),
}
NUMBER = {name: i for i, name in enumerate(KIND)}
HALVES = {"y2a": ("y2", NUMBER["y2"], 0), "y2b": ("y2", len(KIND), 1)}
ONWARD = {
    "m1": (("u", "m2"),), "m2": (("u", "m3"),), "m3": (("y", "n3"),),
    "p1": (("d", "p2"), ("y", "y1")), "p2": (("d", "p3"), ("y", "y2a")), "p3": (("d", "q4"), ("y", "y3")),
    "y0": (("u", "n1"),), "y1": (("d", "y2b"),), "n1": (("u", "n2"),), "y3": (("d", "r4"),),
}
PANEL = {
    "m1": (("y", 0, "n1"),), "p1": (("y", 0, "y1"),),
    "m2": (("z", 1, "m3"), ("y", 0, "n2")), "p2": (("z", -1, "p3"), ("z", -2, "q4"), ("y", 0, "y2")),
    "m3": (("y", 0, "n3"),), "p3": (("y", 0, "y3"),), "q4": (("y", 0, "r4"),),
}
T0, T1, T2 = (1, 0), (1, 1), (1, 2)
BLOCKS = (
    (HERE, HERE), ((0, -1), (0, 2)), ((0, 1), (0, -1)), (T1, (0, -1)),
    (HERE, (0, 1)), ((0, 2), (0, -1)), (T0, HERE), ((0, -2), T1),
    (HERE, (0, -1)), ((0, -2), (0, 2)), ((0, -1), T0), (T1, (0, -2)),
    ((0, -1), (0, 1)), ((0, -1), T1), ((0, 1), T0), ((0, -2), T2),
)
FIRST = (0, 2, 4, 6, 8, 10, 12, 14)
SECOND = (1, 3, 5, 7, 9, 11, 13)
LAST = (15,)
TURN = tuple(2 if n in LAST else n % 2 for n in range(16))


def pick(index, values):
    n = len(values)
    return sum(((n - lax.rem(index - i + n, n)) // n) * value for i, value in enumerate(values) if value)


def kernel(
    scale, x_ref, o_ref, xbuf, pbuf, cbuf, xsum, xrecv, ysend, yrecv, gsend, gtile, abuf, bbuf, fbuf, acc, send_sem, recv_sem
):
    rows, half = x_ref.shape[0], x_ref.shape[0] // 2
    r, c = lax.axis_index("row"), lax.axis_index("col")
    yl, z = r // Z, lax.rem(r, Z)
    x, yh, k = c // (2 * YH), lax.rem(c // 2, YH), lax.rem(c, 2)
    me = yh * X + x
    mine = pl.ds(pl.multiple_of(k * half, half), half)
    other = pl.ds(pl.multiple_of((1 - k) * half, half), half)

    def at_row(side, steps):
        return lax.rem(yl + side, 2) * Z + lax.rem(z + steps + Z, Z)

    def at_col(dx, dy, dk=0):
        return lax.rem(x + dx, X) * (2 * YH) + lax.rem(yh + dy, YH) * 2 + lax.rem(k + dk, 2)

    link = {"u": (at_row(0, 1), c), "d": (at_row(0, -1), c), "y": (at_row(1, 0), c)}
    sibling = (r, at_col(0, 0, 1))

    def block_at(number):
        return at_row(pick(number, [a[0] for a, b in BLOCKS]), pick(number, [a[1] for a, b in BLOCKS])), at_row(
            pick(number, [b[0] for a, b in BLOCKS]), pick(number, [b[1] for a, b in BLOCKS])
        )

    def column(s):
        return lax.rem(s, X) * (2 * YH) + s // X * 2 + k

    to_row, to = block_at(x * YH + yh)
    owner = (to_row, column(to))
    apart = {((b[0] - a[0]) % 2, (b[1] - a[1]) % Z): (n, a) for n, (a, b) in enumerate(BLOCKS)}
    found = [apart[side, steps] for side in range(2) for steps in range(Z)]
    from_me = lax.rem(me // Z - yl + 2, 2) * Z + lax.rem(lax.rem(me, Z) - z + Z, Z)
    from_row = at_row(pick(from_me, [a[0] for n, a in found]), 0 - pick(from_me, [a[1] for n, a in found]))
    source = (from_row, pick(from_me, [n for n, a in found]) * 2 + k)
    at_home = jnp.logical_and(to_row == r, to == me)

    barrier = pltpu.get_barrier_semaphore()
    partners = [*link.values(), sibling]
    partners += [(r, at_col(i, 0)) for i in range(1, X)] + [(r, at_col(0, j)) for j in range(1, YH)]
    for partner in partners:
        pl.semaphore_signal(barrier, inc=1, device_id=partner, device_id_type=MESH)

    @pl.when(jnp.logical_not(at_home))
    def _():
        pl.semaphore_signal(barrier, inc=1, device_id=source, device_id_type=MESH)

    pl.semaphore_wait(barrier, len(partners) + 1 - at_home.astype(jnp.int32))

    def copy(src, dst, sent, received, device):
        return pltpu.make_async_remote_copy(
            src_ref=src, dst_ref=dst, send_sem=send_sem.at[sent], recv_sem=recv_sem.at[received],
            device_id=device, device_id_type=MESH,
        )

    def arrived(dst, received):
        copy(dst, dst, received, received, sibling).wait_recv()

    def left(src, sent):
        copy(src, src, sent, sent, sibling).wait_send()

    def x_part(name, s):
        if name in HALVES:
            kind, number, part = HALVES[name]
            return xbuf.at[s, pl.ds(part * half, half)], X_AT + number
        return xbuf.at[s], X_AT + NUMBER[name]

    def x_wait(*names):
        for name in names:
            arrived(*x_part(name, at_row(*KIND[HALVES[name][0] if name in HALVES else name])))

    def x_onward(name, *only):
        s = at_row(*KIND[name])
        for at, new in ONWARD[name]:
            if not only or new in only:
                part, number = x_part(new, s)
                copy(part, part, number, number, link[at]).start()

    def x_pass(*names):
        for name in names:
            x_wait(name)
            x_onward(name)

    for at, name in (("u", "m1"), ("d", "p1"), ("y", "y0")):
        copy(x_ref, xbuf.at[r], X_AT + NUMBER[name], X_AT + NUMBER[name], link[at]).start()
    xbuf[r] = x_ref[...]

    def gram(n):
        a, b = BLOCKS[n]
        product = lax.dot_general(
            xbuf[at_row(*a)], xbuf[at_row(*b)], (((1,), (1,)), ((), ())), preferred_element_type=jnp.float32
        )
        pbuf[n] = product.astype(jnp.bfloat16)
        copy(pbuf.at[n, other], cbuf.at[n], CORE_AT + n, CORE_AT + n, sibling).start()

    def reduce_x(n):
        arrived(cbuf.at[n], CORE_AT + n)
        total = pbuf[n, mine].astype(jnp.float32) + cbuf[n].astype(jnp.float32)
        xsum[n] = total.astype(jnp.bfloat16)
        to, place = n // YH, n % YH
        apart = lax.rem(x - to + X, X)

        @pl.when(apart != 0)
        def _():
            copy(
                xsum.at[n], xrecv.at[apart, place], XR_AT + n, XR_AT + apart * YH + place,
                (r, to * (2 * YH) + yh * 2 + k),
            ).start()

    def reduce_y(place):
        total = xsum[x * YH + place].astype(jnp.float32)
        for i in range(1, X):
            arrived(xrecv.at[i, place], XR_AT + i * YH + place)
            total = total + xrecv[i, place].astype(jnp.float32)
        ysend[place] = total.astype(jnp.bfloat16)
        apart = lax.rem(yh - place + YH, YH)

        @pl.when(apart != 0)
        def _():
            copy(
                ysend.at[place], yrecv.at[apart], Y_AT + place, Y_AT + apart,
                (r, x * (2 * YH) + place * 2 + k),
            ).start()

    def deliver():
        total = ysend[yh].astype(jnp.float32)
        for j in range(1, YH):
            arrived(yrecv.at[j], Y_AT + j)
            total = total + yrecv[j].astype(jnp.float32)
        gsend[...] = total.astype(jnp.bfloat16)

        @pl.when(jnp.logical_not(at_home))
        def _():
            copy(gsend, gtile, G_AT, G_AT, owner).start()

        @pl.when(at_home)
        def _():
            gtile[...] = gsend[...]

    gram(FIRST[0])
    x_wait("m1")
    x_onward("m1")
    x_wait("p1")
    x_onward("p1")
    x_wait("y0")
    for n in FIRST[1:]:
        gram(n)
    for n in FIRST:
        reduce_x(n)
    x_wait("m2", "p2")
    x_onward("p2", "y2a")
    x_pass("y1")
    x_onward("m2")
    x_onward("y0")
    for n in SECOND:
        gram(n)
    for place in (0, 2):
        reduce_y(place)
    for n in SECOND:
        reduce_x(n)

    @pl.when(lax.rem(yh, 2) == 0)
    def _():
        deliver()

    x_wait("y2a", "y2b")
    for n in LAST:
        gram(n)
    x_onward("p2", "p3")
    for n in LAST:
        reduce_x(n)
    for place in (1, 3):
        reduce_y(place)

    def b_send(at, steps, name, s):
        number = B_AT + NUMBER[name]
        device = link["y"] if at == "y" else (at_row(0, steps), c)
        copy(bbuf.at[s, mine], bbuf.at[s, mine], number, number, device).start()

    def b_share(s):
        copy(bbuf.at[s, mine], bbuf.at[s, mine], BC_AT + s, BC_AT + s, sibling).start()

    def b_pass(*names):
        for name in names:
            s = at_row(*KIND[name])
            arrived(bbuf.at[s, mine], B_AT + NUMBER[name])
            b_share(s)
            for at, steps, new in PANEL.get(name, ()):
                b_send(at, steps, new, s)

    def beside(dx, dy):
        return lax.rem(yh + dy, YH) * X + lax.rem(x + dx, X)

    def a_spread(s, first):
        for i, dx in enumerate((1, 3, 2)):
            copy(abuf.at[s], abuf.at[s], A_AT + first + i, A_AT + s, (r, at_col(dx, 0))).start()

    def a_pass(number, dy):
        s = beside(0, YH - dy)
        arrived(abuf.at[s], A_AT + s)
        a_spread(s, 3 + 3 * number)

    def start():
        @pl.when(jnp.logical_not(at_home))
        def _():
            arrived(gtile, G_AT)

        abuf[me] = gtile[...]
        bbuf[r, mine] = gtile[...]
        for at, steps, name in (("z", 2, "m2"), ("z", -2, "p2"), ("z", 1, "m1"), ("z", -1, "p1"), ("y", 0, "y0")):
            b_send(at, steps, name, r)
        for j, dy in enumerate((1, 3, 2)):
            copy(abuf.at[me], abuf.at[me], A_AT + j, A_AT + me, (r, at_col(0, dy))).start()
        a_spread(me, 3)
        b_share(r)

    def turn(side, steps):
        return pick(lax.rem(side + 2, 2) * Z + lax.rem(steps + 2 * Z, Z), [TURN[n] for n, a in found])

    def turn_of(row, s):
        return turn(s // Z - row // Z, lax.rem(s, Z) - lax.rem(row, Z))

    def panels(now):
        for name in ("m1", "p1", "m2", "p2"):
            pl.when(turn_of(at_row(*KIND[name]), me) == now)(functools.partial(b_pass, name))
        for number, dy in enumerate((1, 3, 2), 1):
            pl.when(turn_of(r, beside(0, YH - dy)) == now)(functools.partial(a_pass, number, dy))
        for name in ("m3", "p3", "q4"):
            pl.when(turn_of(at_row(*KIND[name]), me) == now)(functools.partial(b_pass, name))

    mine_is = turn_of(r, me)
    pl.when(mine_is == 0)(start)
    x_pass("m3", "n1")

    @pl.when(lax.rem(yh, 2) == 1)
    def _():
        deliver()

    panels(0)
    x_pass("p3")
    pl.when(mine_is == 1)(start)
    pl.when(mine_is == 2)(start)
    panels(1)
    x_pass("y3")
    panels(2)
    b_pass("y0", "n1", "y1", "n2", "y2", "n3", "y3", "r4")
    for dx in (1, 3, 2):
        for dy in range(YH):
            s = beside(dx, dy)
            arrived(abuf.at[s], A_AT + s)

    squared = jnp.zeros((half, rows), jnp.float32)
    for s in range(N_ROW):
        arrived(bbuf.at[s, other], BC_AT + s)
        squared = squared + jnp.dot(abuf[s], bbuf[s], preferred_element_type=jnp.float32)
    fbuf[me, mine] = (coef_b * gtile[...].astype(jnp.float32) + coef_c * squared).astype(jnp.bfloat16)

    def f_share(s):
        copy(fbuf.at[s, mine], fbuf.at[s, mine], FC_AT + s, FC_AT + s, sibling).start()

    def f_spread(s, first):
        for i, dx in enumerate((1, 3, 2)):
            copy(
                fbuf.at[s, mine], fbuf.at[s, mine], F_AT + first + i, F_AT + s, (r, at_col(dx, 0))
            ).start()

    def f_apply(dx):
        for dy in range(YH):
            s = beside(dx, dy)
            arrived(fbuf.at[s, other], FC_AT + s)
            acc[...] += jnp.dot(fbuf[s], xbuf[s], preferred_element_type=jnp.float32)

    for j, dy in enumerate((1, 3, 2)):
        copy(fbuf.at[me, mine], fbuf.at[me, mine], F_AT + j, F_AT + me, (r, at_col(0, dy))).start()
    f_spread(me, 3)
    f_share(me)
    acc[...] = coef_a * x_ref[...].astype(jnp.float32)
    for name in ("q4", "n2", "n3", "r4"):
        x_wait(name)
    for j, dy in enumerate((1, 3, 2)):
        s = beside(0, YH - dy)
        arrived(fbuf.at[s, mine], F_AT + s)
        f_share(s)
        f_spread(s, 6 + 3 * j)
    done = 0
    for dx in (1, 3, 2):
        for dy in range(YH):
            s = beside(dx, dy)
            arrived(fbuf.at[s, mine], F_AT + s)
            f_share(s)
        f_apply(done)
        done = dx
    f_apply(done)
    o_ref[...] = (scale * acc[...]).astype(o_ref.dtype)

    for number in range(16):
        split = number in [n for kind, n, part in HALVES.values()]
        left(x_ref.at[pl.ds(0, half)] if split else x_ref, X_AT + number)
    for number in range(15):
        left(abuf.at[0], A_AT + number)
        left(abuf.at[0], B_AT + number)
        left(abuf.at[0], F_AT + number)
    for place in range(YH):

        @pl.when(yh != place)
        def _():
            left(ysend.at[place], Y_AT + place)

    @pl.when(jnp.logical_not(at_home))
    def _():
        left(gsend, G_AT)

    def all_left(s, carry):
        left(cbuf.at[s], CORE_AT + s)
        left(cbuf.at[s], BC_AT + s)
        left(cbuf.at[s], FC_AT + s)

        @pl.when(s // YH != x)
        def _():
            left(xsum.at[s], XR_AT + s)

        return carry

    lax.fori_loop(0, N_ROW, all_left, 0)


def solution(mesh):
    def step(iterate):
        rows, width = iterate.shape
        half, n = rows // 2, width * mesh.shape["col"]
        bf16 = jnp.bfloat16

        def body(*refs):
            kernel(math.sqrt(n), *refs)

        return pl.pallas_call(
            body,
            out_shape=jax.ShapeDtypeStruct((rows, width), bf16),
            in_specs=[pl.BlockSpec(memory_space=pltpu.VMEM)],
            out_specs=pl.BlockSpec(memory_space=pltpu.VMEM),
            scratch_shapes=[
                pltpu.VMEM((N_ROW, rows, width), bf16),
                pltpu.VMEM((N_ROW, rows, rows), bf16),
                pltpu.VMEM((N_ROW, half, rows), bf16),
                pltpu.VMEM((N_ROW, half, rows), bf16),
                pltpu.VMEM((X, YH, half, rows), bf16),
                pltpu.VMEM((YH, half, rows), bf16),
                pltpu.VMEM((YH, half, rows), bf16),
                pltpu.VMEM((half, rows), bf16),
                pltpu.VMEM((half, rows), bf16),
                pltpu.VMEM((N_ROW, half, rows), bf16),
                pltpu.VMEM((N_ROW, rows, rows), bf16),
                pltpu.VMEM((N_ROW, rows, rows), bf16),
                pltpu.VMEM((rows, width), jnp.float32),
                pltpu.SemaphoreType.DMA((N_SEM,)),
                pltpu.SemaphoreType.DMA((N_SEM,)),
            ],
            compiler_params=pltpu.CompilerParams(
                collective_id=0, has_side_effects=True, vmem_limit_bytes=48 << 20
            ),
            cost_estimate=pl.CostEstimate(
                flops=2 * rows * N_ROW * rows * (2 * width + half), bytes_accessed=4 * rows * width, transcendentals=0
            ),
        )(iterate)

    return jax.shard_map(
        step, mesh=mesh, in_specs=(P("row", "col"),), out_specs=P("row", "col"), check_vma=False
    )
```

```python
import functools
import math

import jax
import jax.numpy as jnp
from jax import lax
from jax.experimental import pallas as pl
from jax.experimental.pallas import tpu as pltpu
from jax.sharding import PartitionSpec as P

MESH = pl.DeviceIdType.MESH
coef_a = 3.4445
coef_b = -4.775
coef_c = 2.0315

Z, X, YH = 8, 4, 4
N_ROW = 2 * Z

X_AT = 0
CORE_AT = X_AT + 45
XR_AT = CORE_AT + 16
Y_AT = XR_AT + 16
G_AT = Y_AT + 4
A_AT = G_AT + 1
B_AT = A_AT + 16
BC_AT = B_AT + 15
F_AT = BC_AT + 16
FC_AT = F_AT + 16
N_SEM = FC_AT + 16

HERE = (0, 0)
KIND = {
    "m1": (0, -1), "m2": (0, -2), "m3": (0, -3), "p1": (0, 1), "p2": (0, 2), "p3": (0, 3), "q4": (0, 4),
    "y0": (1, 0), "y1": (1, 1), "y2": (1, 2), "y3": (1, 3), "r4": (1, 4), "n1": (1, -1), "n2": (1, -2), "n3": (1, -3),
}
NUMBER = {name: i for i, name in enumerate(KIND)}
MAIN, CUT = 512, 128
BOTH = (0, 1)
ONWARD = {
    "m1": (("u", "m2", BOTH),), "m2": (("u", "m3", BOTH),),
    "p1": (("d", "p2", BOTH), ("y", "y1", BOTH)), "p2": (("d", "p3", BOTH), ("y", "y2", (0,))),
    "p3": (("d", "q4", BOTH), ("y", "y3", BOTH)),
    "y0": (("u", "n1", BOTH),), "y1": (("d", "y2", (1,)),), "y3": (("d", "r4", BOTH),),
    "n1": (("u", "n2", BOTH),), "n2": (("u", "n3", BOTH),),
}
PANEL = {
    "m1": (("y", 0, "n1"),), "p1": (("y", 0, "y1"),),
    "m2": (("z", 1, "m3"), ("y", 0, "n2")), "p2": (("z", -1, "p3"), ("z", -2, "q4"), ("y", 0, "y2")),
    "m3": (("y", 0, "n3"),), "p3": (("y", 0, "y3"),), "q4": (("y", 0, "r4"),),
}
T0, T1, T2 = (1, 0), (1, 1), (1, 2)
BLOCKS = (
    (HERE, HERE), ((0, -1), (0, 2)), ((0, 1), (0, -1)), (T1, (0, -1)),
    (HERE, (0, 1)), ((0, 2), (0, -1)), (T0, HERE), ((0, -2), T1),
    (HERE, (0, -1)), ((0, -2), (0, 2)), ((0, -1), T0), (T1, (0, -2)),
    ((0, -1), (0, 1)), ((0, -1), T1), ((0, 1), T0), ((0, -2), T2),
)
FIRST = (0, 2, 4, 6, 8, 10, 12, 14)
SECOND = (1, 3, 5, 7, 9, 11, 13)
LAST = (15,)


def pick(index, values):
    n = len(values)
    return sum(((n - lax.rem(index - i + n, n)) // n) * value for i, value in enumerate(values) if value)


def kernel(
    scale, x_ref, o_ref, xown, xmain, xpack, xtail, pbuf, cbuf, xsum, xrecv, ysend, yrecv, gsend, gtile, abuf, bbuf, fbuf, acc, fetch_sem, send_sem, recv_sem
):
    rows, width = x_ref.shape
    half = rows // 2
    r, c = lax.axis_index("row"), lax.axis_index("col")
    yl, z = r // Z, lax.rem(r, Z)
    x, yh, k = c // (2 * YH), lax.rem(c // 2, YH), lax.rem(c, 2)
    me = yh * X + x
    mine = pl.ds(pl.multiple_of(k * half, half), half)
    other = pl.ds(pl.multiple_of((1 - k) * half, half), half)

    def at_row(side, steps):
        return lax.rem(yl + side, 2) * Z + lax.rem(z + steps + Z, Z)

    def at_col(dx, dy, dk=0):
        return lax.rem(x + dx, X) * (2 * YH) + lax.rem(yh + dy, YH) * 2 + lax.rem(k + dk, 2)

    link = {"u": (at_row(0, 1), c), "d": (at_row(0, -1), c), "y": (at_row(1, 0), c)}
    sibling = (r, at_col(0, 0, 1))

    def block_at(number):
        return at_row(pick(number, [a[0] for a, b in BLOCKS]), pick(number, [a[1] for a, b in BLOCKS])), at_row(
            pick(number, [b[0] for a, b in BLOCKS]), pick(number, [b[1] for a, b in BLOCKS])
        )

    def column(s):
        return lax.rem(s, X) * (2 * YH) + s // X * 2 + k

    to_row, to = block_at(x * YH + yh)
    owner = (to_row, column(to))
    apart = {((b[0] - a[0]) % 2, (b[1] - a[1]) % Z): (n, a) for n, (a, b) in enumerate(BLOCKS)}
    found = [apart[side, steps] for side in range(2) for steps in range(Z)]
    from_me = lax.rem(me // Z - yl + 2, 2) * Z + lax.rem(lax.rem(me, Z) - z + Z, Z)
    from_row = at_row(pick(from_me, [a[0] for n, a in found]), 0 - pick(from_me, [a[1] for n, a in found]))
    source = (from_row, pick(from_me, [n for n, a in found]) * 2 + k)
    at_home = jnp.logical_and(to_row == r, to == me)

    fetch = pltpu.make_async_copy(x_ref, xown, fetch_sem)
    fetch.start()
    barrier = pltpu.get_barrier_semaphore()
    partners = [*link.values(), sibling]
    partners += [(r, at_col(i, 0)) for i in range(1, X)] + [(r, at_col(0, j)) for j in range(1, YH)]
    for partner in partners:
        pl.semaphore_signal(barrier, inc=1, device_id=partner, device_id_type=MESH)

    @pl.when(jnp.logical_not(at_home))
    def _():
        pl.semaphore_signal(barrier, inc=1, device_id=source, device_id_type=MESH)

    pl.semaphore_wait(barrier, len(partners) + 1 - at_home.astype(jnp.int32))

    def copy(src, dst, sent, received, device):
        return pltpu.make_async_remote_copy(
            src_ref=src, dst_ref=dst, send_sem=send_sem.at[sent], recv_sem=recv_sem.at[received],
            device_id=device, device_id_type=MESH,
        )

    def arrived(dst, received):
        copy(dst, dst, received, received, sibling).wait_recv()

    def left(src, sent):
        copy(src, src, sent, sent, sibling).wait_send()

    side = width - MAIN

    def pack(s):
        xpack[s, :, pl.ds(0, side)] = xtail[s, pl.ds(0, half), :]
        xpack[s, :, pl.ds(side, side)] = xtail[s, pl.ds(half, half), :]

    def unpack(*names):
        for name in names:
            s = at_row(*KIND[name])
            xtail[s, pl.ds(0, half), :] = xpack[s, :, pl.ds(0, side)]
            xtail[s, pl.ds(half, half), :] = xpack[s, :, pl.ds(side, side)]

    def x_pieces(name, s, part):
        number = X_AT + 3 * NUMBER[name]
        if part == 0:
            return [(xmain.at[s, pl.ds(0, CUT)], number)]
        return [(xmain.at[s, pl.ds(CUT, rows - CUT)], number + 1), (xpack.at[s], number + 2)]

    def x_send(at, name, s, part):
        for piece, number in x_pieces(name, s, part):
            copy(piece, piece, number, number, link[at]).start()

    def x_wait(name, part):
        for piece, number in x_pieces(name, at_row(*KIND[name]), part):
            arrived(piece, number)

    def x_onward(name, part, *only):
        for at, new, parts in ONWARD[name]:
            if part in parts and (not only or new in only):
                x_send(at, new, at_row(*KIND[name]), part)

    def x_pass(*names):
        for part in BOTH:
            for name in names:
                x_wait(name, part)
                x_onward(name, part)

    fetch.wait()
    xmain[r] = xown[:, pl.ds(0, MAIN)]
    xtail[r] = xown[:, pl.ds(MAIN, side)]
    pack(r)
    for part in BOTH:
        for at, name in (("u", "m1"), ("d", "p1"), ("y", "y0")):
            x_send(at, name, r, part)

    def gram(n):
        a, b = BLOCKS[n]
        a, b = at_row(*a), at_row(*b)
        across = (((1,), (1,)), ((), ()))
        product = lax.dot_general(xmain[a], xmain[b], across, preferred_element_type=jnp.float32)
        product = product + lax.dot_general(xtail[a], xtail[b], across, preferred_element_type=jnp.float32)
        pbuf[n] = product.astype(jnp.bfloat16)
        copy(pbuf.at[n, other], cbuf.at[n], CORE_AT + n, CORE_AT + n, sibling).start()

    def reduce_x(n):
        arrived(cbuf.at[n], CORE_AT + n)
        total = pbuf[n, mine].astype(jnp.float32) + cbuf[n].astype(jnp.float32)
        xsum[n] = total.astype(jnp.bfloat16)
        to, place = n // YH, n % YH
        apart = lax.rem(x - to + X, X)

        @pl.when(apart != 0)
        def _():
            copy(
                xsum.at[n], xrecv.at[apart, place], XR_AT + n, XR_AT + apart * YH + place,
                (r, to * (2 * YH) + yh * 2 + k),
            ).start()

    def grams_and_sums(numbers, before):
        pending = list(before)
        for n in numbers:
            gram(n)
            pending.append(n)
            if len(pending) > 3:
                reduce_x(pending.pop(0))
        for n in pending:
            reduce_x(n)

    def reduce_y(place):
        total = xsum[x * YH + place].astype(jnp.float32)
        for i in range(1, X):
            arrived(xrecv.at[i, place], XR_AT + i * YH + place)
            total = total + xrecv[i, place].astype(jnp.float32)
        ysend[place] = total.astype(jnp.bfloat16)
        apart = lax.rem(yh - place + YH, YH)

        @pl.when(apart != 0)
        def _():
            copy(
                ysend.at[place], yrecv.at[apart], Y_AT + place, Y_AT + apart,
                (r, x * (2 * YH) + place * 2 + k),
            ).start()

    def deliver():
        total = ysend[yh].astype(jnp.float32)
        for j in range(1, YH):
            arrived(yrecv.at[j], Y_AT + j)
            total = total + yrecv[j].astype(jnp.float32)
        gsend[...] = total.astype(jnp.bfloat16)

        @pl.when(jnp.logical_not(at_home))
        def _():
            copy(gsend, gtile, G_AT, G_AT, owner).start()

        @pl.when(at_home)
        def _():
            gtile[...] = gsend[...]

    gram(FIRST[0])
    for part in BOTH:
        for name in ("m1", "p1", "y0"):
            x_wait(name, part)
            if name != "y0":
                x_onward(name, part)
    unpack("m1", "p1", "y0")
    grams_and_sums(FIRST[1:], FIRST[:1])
    for part in BOTH:
        x_wait("m2", part)
        x_wait("p2", part)
        x_onward("p2", part, "y2")
        x_wait("y1", part)
        x_onward("y1", part)
    for part in BOTH:
        x_onward("m2", part)
        x_onward("y0", part)
    unpack("m2", "p2", "y1")
    grams_and_sums(SECOND, ())
    for place in (0, 2):
        reduce_y(place)
    for part in BOTH:
        x_wait("y2", part)
    unpack("y2")
    for n in LAST:
        gram(n)
    for part in BOTH:
        x_onward("p2", part, "p3")
    for n in LAST:
        reduce_x(n)

    @pl.when(lax.rem(yh, 2) == 0)
    def _():
        deliver()

    for place in (1, 3):
        reduce_y(place)

    def b_send(at, steps, name, s):
        number = B_AT + NUMBER[name]
        device = link["y"] if at == "y" else (at_row(0, steps), c)
        copy(bbuf.at[s, mine], bbuf.at[s, mine], number, number, device).start()

    def b_share(s):
        copy(bbuf.at[s, mine], bbuf.at[s, mine], BC_AT + s, BC_AT + s, sibling).start()

    def b_pass(*names):
        for name in names:
            s = at_row(*KIND[name])
            arrived(bbuf.at[s, mine], B_AT + NUMBER[name])
            b_share(s)
            for at, steps, new in PANEL.get(name, ()):
                b_send(at, steps, new, s)

    def beside(dx, dy):
        return lax.rem(yh + dy, YH) * X + lax.rem(x + dx, X)

    def a_spread(s, first):
        for i, dx in enumerate((1, 3, 2)):
            copy(abuf.at[s], abuf.at[s], A_AT + first + i, A_AT + s, (r, at_col(dx, 0))).start()

    def a_pass(number, dy):
        s = beside(0, YH - dy)
        arrived(abuf.at[s], A_AT + s)
        a_spread(s, 3 + 3 * number)

    x_pass("n1", "p3")

    @pl.when(lax.rem(yh, 2) == 1)
    def _():
        deliver()


    @pl.when(jnp.logical_not(at_home))
    def _():
        arrived(gtile, G_AT)

    abuf[me] = gtile[...]
    bbuf[r, mine] = gtile[...]
    for at, steps, name in (("z", 2, "m2"), ("z", -2, "p2"), ("z", 1, "m1"), ("z", -1, "p1"), ("y", 0, "y0")):
        b_send(at, steps, name, r)
    for j, dy in enumerate((1, 3, 2)):
        copy(abuf.at[me], abuf.at[me], A_AT + j, A_AT + me, (r, at_col(0, dy))).start()
    a_spread(me, 3)
    b_share(r)
    b_pass("m1", "p1", "m2", "p2")
    a_pass(1, 1)
    a_pass(2, 3)
    a_pass(3, 2)
    x_pass("y3", "n2")
    b_pass("m3", "p3", "q4", "y0", "n1", "y1", "n2", "y2", "n3", "y3", "r4")
    for dx in (1, 3, 2):
        for dy in range(YH):
            s = beside(dx, dy)
            arrived(abuf.at[s], A_AT + s)

    squared = jnp.zeros((half, rows), jnp.float32)
    for s in range(N_ROW):
        arrived(bbuf.at[s, other], BC_AT + s)
        squared = squared + jnp.dot(abuf[s], bbuf[s], preferred_element_type=jnp.float32)
    fbuf[me, mine] = (coef_b * gtile[...].astype(jnp.float32) + coef_c * squared).astype(jnp.bfloat16)

    def f_share(s):
        copy(fbuf.at[s, mine], fbuf.at[s, mine], FC_AT + s, FC_AT + s, sibling).start()

    def f_spread(s, first):
        for i, dx in enumerate((1, 3, 2)):
            copy(
                fbuf.at[s, mine], fbuf.at[s, mine], F_AT + first + i, F_AT + s, (r, at_col(dx, 0))
            ).start()

    def f_apply(dx):
        for dy in range(YH):
            s = beside(dx, dy)
            arrived(fbuf.at[s, other], FC_AT + s)
            acc[:, pl.ds(0, MAIN)] += jnp.dot(fbuf[s], xmain[s], preferred_element_type=jnp.float32)
            acc[:, pl.ds(MAIN, side)] += jnp.dot(fbuf[s], xtail[s], preferred_element_type=jnp.float32)

    for j, dy in enumerate((1, 3, 2)):
        copy(fbuf.at[me, mine], fbuf.at[me, mine], F_AT + j, F_AT + me, (r, at_col(0, dy))).start()
    f_spread(me, 3)
    f_share(me)
    acc[...] = coef_a * xown[...].astype(jnp.float32)
    for name in ("m3", "q4", "n3", "r4"):
        for part in BOTH:
            x_wait(name, part)
    unpack("m3", "p3", "q4", "y3", "n1", "n2", "n3", "r4")
    for j, dy in enumerate((1, 3, 2)):
        s = beside(0, YH - dy)
        arrived(fbuf.at[s, mine], F_AT + s)
        f_share(s)
        f_spread(s, 6 + 3 * j)
    done = 0
    for dx in (1, 3, 2):
        for dy in range(YH):
            s = beside(dx, dy)
            arrived(fbuf.at[s, mine], F_AT + s)
            f_share(s)
        f_apply(done)
        done = dx
    f_apply(done)
    o_ref[...] = (scale * acc[...]).astype(o_ref.dtype)

    for name in KIND:
        for part in BOTH:
            for piece, number in x_pieces(name, 0, part):
                left(piece, number)
    for number in range(15):
        left(abuf.at[0], A_AT + number)
        left(abuf.at[0], B_AT + number)
        left(abuf.at[0], F_AT + number)
    for place in range(YH):

        @pl.when(yh != place)
        def _():
            left(ysend.at[place], Y_AT + place)

    @pl.when(jnp.logical_not(at_home))
    def _():
        left(gsend, G_AT)

    def all_left(s, carry):
        left(cbuf.at[s], CORE_AT + s)
        left(cbuf.at[s], BC_AT + s)
        left(cbuf.at[s], FC_AT + s)

        @pl.when(s // YH != x)
        def _():
            left(xsum.at[s], XR_AT + s)

        return carry

    lax.fori_loop(0, N_ROW, all_left, 0)


def solution(mesh):
    def step(iterate):
        rows, width = iterate.shape
        half, n = rows // 2, width * mesh.shape["col"]
        bf16 = jnp.bfloat16

        def body(*refs):
            kernel(math.sqrt(n), *refs)

        return pl.pallas_call(
            body,
            out_shape=jax.ShapeDtypeStruct((rows, width), bf16),
            in_specs=[pl.BlockSpec(memory_space=pl.ANY)],
            out_specs=pl.BlockSpec(memory_space=pltpu.VMEM),
            scratch_shapes=[
                pltpu.VMEM((rows, width), bf16),
                pltpu.VMEM((N_ROW, rows, MAIN), bf16),
                pltpu.VMEM((N_ROW, half, 2 * (width - MAIN)), bf16),
                pltpu.VMEM((N_ROW, rows, width - MAIN), bf16),
                pltpu.VMEM((N_ROW, rows, rows), bf16),
                pltpu.VMEM((N_ROW, half, rows), bf16),
                pltpu.VMEM((N_ROW, half, rows), bf16),
                pltpu.VMEM((X, YH, half, rows), bf16),
                pltpu.VMEM((YH, half, rows), bf16),
                pltpu.VMEM((YH, half, rows), bf16),
                pltpu.VMEM((half, rows), bf16),
                pltpu.VMEM((half, rows), bf16),
                pltpu.VMEM((N_ROW, half, rows), bf16),
                pltpu.VMEM((N_ROW, rows, rows), bf16),
                pltpu.VMEM((N_ROW, rows, rows), bf16),
                pltpu.VMEM((rows, width), jnp.float32),
                pltpu.SemaphoreType.DMA(()),
                pltpu.SemaphoreType.DMA((N_SEM,)),
                pltpu.SemaphoreType.DMA((N_SEM,)),
            ],
            compiler_params=pltpu.CompilerParams(
                collective_id=0, has_side_effects=True, vmem_limit_bytes=48 << 20
            ),
            cost_estimate=pl.CostEstimate(
                flops=2 * rows * N_ROW * rows * (2 * width + half), bytes_accessed=4 * rows * width, transcendentals=0
            ),
        )(iterate)

    return jax.shard_map(
        step, mesh=mesh, in_specs=(P("row", "col"),), out_specs=P("row", "col"), check_vma=False
    )
```

```python
import functools
import math

import jax
import jax.numpy as jnp
from jax import lax
from jax.experimental import pallas as pl
from jax.experimental.pallas import tpu as pltpu
from jax.sharding import PartitionSpec as P

MESH = pl.DeviceIdType.MESH
coef_a = 3.4445
coef_b = -4.775
coef_c = 2.0315

Z, X, YH = 8, 4, 4
N_ROW = 2 * Z

X_AT = 0
CORE_AT = X_AT + 45
XR_AT = CORE_AT + 16
Y_AT = XR_AT + 16
G_AT = Y_AT + 4
A_AT = G_AT + 1
B_AT = A_AT + 16
BC_AT = B_AT + 15
F_AT = BC_AT + 16
FC_AT = F_AT + 16
N_SEM = FC_AT + 16

HERE = (0, 0)
KIND = {
    "m1": (0, -1), "m2": (0, -2), "m3": (0, -3), "p1": (0, 1), "p2": (0, 2), "p3": (0, 3), "q4": (0, 4),
    "y0": (1, 0), "y1": (1, 1), "y2": (1, 2), "y3": (1, 3), "r4": (1, 4), "n1": (1, -1), "n2": (1, -2), "n3": (1, -3),
}
NUMBER = {name: i for i, name in enumerate(KIND)}
MAIN, CUT = 512, 128
BOTH = (0, 1)
ONWARD = {
    "m1": (("u", "m2", BOTH),), "m2": (("u", "m3", BOTH),),
    "p1": (("d", "p2", BOTH), ("y", "y1", BOTH)), "p2": (("d", "p3", BOTH), ("y", "y2", (0,))),
    "p3": (("d", "q4", BOTH), ("y", "y3", BOTH)),
    "y0": (("u", "n1", BOTH),), "y1": (("d", "y2", (1,)),), "y3": (("d", "r4", BOTH),),
    "n1": (("u", "n2", BOTH),), "n2": (("u", "n3", BOTH),),
}
PANEL = {
    "m1": (("y", 0, "n1"),), "p1": (("y", 0, "y1"),),
    "m2": (("z", 1, "m3"), ("y", 0, "n2")), "p2": (("z", -1, "p3"), ("z", -2, "q4"), ("y", 0, "y2")),
    "m3": (("y", 0, "n3"),), "p3": (("y", 0, "y3"),), "q4": (("y", 0, "r4"),),
}
T0, T1, T2 = (1, 0), (1, 1), (1, 2)
BLOCKS = (
    (HERE, HERE), ((0, -1), (0, 2)), ((0, 1), (0, -1)), (T1, (0, -1)),
    (HERE, (0, 1)), ((0, 2), (0, -1)), (T0, HERE), ((0, -2), T1),
    (HERE, (0, -1)), ((0, -2), (0, 2)), ((0, -1), T0), (T1, (0, -2)),
    ((0, -1), (0, 1)), ((0, -1), T1), ((0, 1), T0), ((0, -2), T2),
)
FIRST = (0, 2, 4, 6, 8, 10, 12, 14)
SECOND = (1, 3, 5, 7, 9, 11, 13)
LAST = (15,)


def pick(index, values):
    n = len(values)
    return sum(((n - lax.rem(index - i + n, n)) // n) * value for i, value in enumerate(values) if value)


def kernel(
    scale, x_ref, o_ref, xown, xmain, xpack, xtail, pbuf, cbuf, xsum, xrecv, ysend, yrecv, gsend, gtile, abuf, bbuf, fbuf, acc, fetch_sem, send_sem, recv_sem
):
    rows, width = x_ref.shape
    half = rows // 2
    r, c = lax.axis_index("row"), lax.axis_index("col")
    yl, z = r // Z, lax.rem(r, Z)
    x, yh, k = c // (2 * YH), lax.rem(c // 2, YH), lax.rem(c, 2)
    me = yh * X + x
    mine = pl.ds(pl.multiple_of(k * half, half), half)
    other = pl.ds(pl.multiple_of((1 - k) * half, half), half)

    def at_row(side, steps):
        return lax.rem(yl + side, 2) * Z + lax.rem(z + steps + Z, Z)

    def at_col(dx, dy, dk=0):
        return lax.rem(x + dx, X) * (2 * YH) + lax.rem(yh + dy, YH) * 2 + lax.rem(k + dk, 2)

    link = {"u": (at_row(0, 1), c), "d": (at_row(0, -1), c), "y": (at_row(1, 0), c)}
    sibling = (r, at_col(0, 0, 1))

    def block_at(number):
        return at_row(pick(number, [a[0] for a, b in BLOCKS]), pick(number, [a[1] for a, b in BLOCKS])), at_row(
            pick(number, [b[0] for a, b in BLOCKS]), pick(number, [b[1] for a, b in BLOCKS])
        )

    def column(s):
        return lax.rem(s, X) * (2 * YH) + s // X * 2 + k

    to_row, to = block_at(x * YH + yh)
    owner = (to_row, column(to))
    at_home = jnp.logical_and(to_row == r, to == me)

    fetch = pltpu.make_async_copy(x_ref, xown, fetch_sem)
    fetch.start()
    barrier = pltpu.get_barrier_semaphore()
    partners = [*link.values(), sibling]
    partners += [(r, at_col(i, 0)) for i in range(1, X)] + [(r, at_col(0, j)) for j in range(1, YH)]
    for partner in partners:
        pl.semaphore_signal(barrier, inc=1, device_id=partner, device_id_type=MESH)

    pl.semaphore_wait(barrier, len(partners))

    def copy(src, dst, sent, received, device):
        return pltpu.make_async_remote_copy(
            src_ref=src, dst_ref=dst, send_sem=send_sem.at[sent], recv_sem=recv_sem.at[received],
            device_id=device, device_id_type=MESH,
        )

    def arrived(dst, received):
        copy(dst, dst, received, received, sibling).wait_recv()

    def left(src, sent):
        copy(src, src, sent, sent, sibling).wait_send()

    side = width - MAIN

    def pack(s):
        xpack[s, :, pl.ds(0, side)] = xtail[s, pl.ds(0, half), :]
        xpack[s, :, pl.ds(side, side)] = xtail[s, pl.ds(half, half), :]

    def unpack(*names):
        for name in names:
            s = at_row(*KIND[name])
            xtail[s, pl.ds(0, half), :] = xpack[s, :, pl.ds(0, side)]
            xtail[s, pl.ds(half, half), :] = xpack[s, :, pl.ds(side, side)]

    def x_pieces(name, s, part):
        number = X_AT + 3 * NUMBER[name]
        if part == 0:
            return [(xmain.at[s, pl.ds(0, CUT)], number)]
        return [(xmain.at[s, pl.ds(CUT, rows - CUT)], number + 1), (xpack.at[s], number + 2)]

    def x_send(at, name, s, part):
        for piece, number in x_pieces(name, s, part):
            copy(piece, piece, number, number, link[at]).start()

    def x_wait(name, part):
        for piece, number in x_pieces(name, at_row(*KIND[name]), part):
            arrived(piece, number)

    def x_onward(name, part, *only):
        for at, new, parts in ONWARD[name]:
            if part in parts and (not only or new in only):
                x_send(at, new, at_row(*KIND[name]), part)

    def x_pass(*names):
        for part in BOTH:
            for name in names:
                x_wait(name, part)
                x_onward(name, part)

    fetch.wait()
    xmain[r] = xown[:, pl.ds(0, MAIN)]
    xtail[r] = xown[:, pl.ds(MAIN, side)]
    pack(r)
    for part in BOTH:
        for at, name in (("u", "m1"), ("d", "p1"), ("y", "y0")):
            x_send(at, name, r, part)

    def gram(n):
        a, b = BLOCKS[n]
        a, b = at_row(*a), at_row(*b)
        across = (((1,), (1,)), ((), ()))
        product = lax.dot_general(xmain[a], xmain[b], across, preferred_element_type=jnp.float32)
        product = product + lax.dot_general(xtail[a], xtail[b], across, preferred_element_type=jnp.float32)
        pbuf[n] = product.astype(jnp.bfloat16)
        copy(pbuf.at[n, other], cbuf.at[n], CORE_AT + n, CORE_AT + n, sibling).start()

    def reduce_x(n):
        arrived(cbuf.at[n], CORE_AT + n)
        total = pbuf[n, mine].astype(jnp.float32) + cbuf[n].astype(jnp.float32)
        xsum[n] = total.astype(jnp.bfloat16)
        to, place = n // YH, n % YH
        apart = lax.rem(x - to + X, X)

        @pl.when(apart != 0)
        def _():
            copy(
                xsum.at[n], xrecv.at[apart, place], XR_AT + n, XR_AT + apart * YH + place,
                (r, to * (2 * YH) + yh * 2 + k),
            ).start()

    def grams_and_sums(numbers, before):
        pending = list(before)
        for n in numbers:
            gram(n)
            pending.append(n)
            if len(pending) > 3:
                reduce_x(pending.pop(0))
        for n in pending:
            reduce_x(n)

    def reduce_y(place):
        total = xsum[x * YH + place].astype(jnp.float32)
        for i in range(1, X):
            arrived(xrecv.at[i, place], XR_AT + i * YH + place)
            total = total + xrecv[i, place].astype(jnp.float32)
        ysend[place] = total.astype(jnp.bfloat16)
        apart = lax.rem(yh - place + YH, YH)

        @pl.when(apart != 0)
        def _():
            copy(
                ysend.at[place], yrecv.at[apart], Y_AT + place, Y_AT + apart,
                (r, x * (2 * YH) + place * 2 + k),
            ).start()

    def deliver():
        total = ysend[yh].astype(jnp.float32)
        for j in range(1, YH):
            arrived(yrecv.at[j], Y_AT + j)
            total = total + yrecv[j].astype(jnp.float32)
        gsend[...] = total.astype(jnp.bfloat16)

        @pl.when(jnp.logical_not(at_home))
        def _():
            copy(gsend, gtile, G_AT, G_AT, owner).start()

        @pl.when(at_home)
        def _():
            gtile[...] = gsend[...]

    gram(FIRST[0])
    for part in BOTH:
        for name in ("m1", "p1", "y0"):
            x_wait(name, part)
            if name != "y0":
                x_onward(name, part)
    unpack("m1", "p1", "y0")
    grams_and_sums(FIRST[1:], FIRST[:1])
    for part in BOTH:
        x_wait("m2", part)
        x_wait("p2", part)
        x_onward("p2", part, "y2")
        x_wait("y1", part)
        x_onward("y1", part)
    for part in BOTH:
        x_onward("m2", part)
        x_onward("y0", part)
    unpack("m2", "p2", "y1")
    grams_and_sums(SECOND, ())
    for place in (0, 2):
        reduce_y(place)
    for part in BOTH:
        x_wait("y2", part)
    unpack("y2")
    for n in LAST:
        gram(n)
    for part in BOTH:
        x_onward("p2", part, "p3")
    for n in LAST:
        reduce_x(n)

    @pl.when(lax.rem(yh, 2) == 0)
    def _():
        deliver()

    for place in (1, 3):
        reduce_y(place)

    def b_send(at, steps, name, s):
        number = B_AT + NUMBER[name]
        device = link["y"] if at == "y" else (at_row(0, steps), c)
        copy(bbuf.at[s, mine], bbuf.at[s, mine], number, number, device).start()

    def b_share(s):
        copy(bbuf.at[s, mine], bbuf.at[s, mine], BC_AT + s, BC_AT + s, sibling).start()

    def b_pass(*names):
        for name in names:
            s = at_row(*KIND[name])
            arrived(bbuf.at[s, mine], B_AT + NUMBER[name])
            b_share(s)
            for at, steps, new in PANEL.get(name, ()):
                b_send(at, steps, new, s)

    def beside(dx, dy):
        return lax.rem(yh + dy, YH) * X + lax.rem(x + dx, X)

    def a_spread(s, first):
        for i, dx in enumerate((1, 3, 2)):
            copy(abuf.at[s], abuf.at[s], A_AT + first + i, A_AT + s, (r, at_col(dx, 0))).start()

    def a_pass(number, dy):
        s = beside(0, YH - dy)
        arrived(abuf.at[s], A_AT + s)
        a_spread(s, 3 + 3 * number)

    x_pass("n1", "p3")

    @pl.when(lax.rem(yh, 2) == 1)
    def _():
        deliver()


    @pl.when(jnp.logical_not(at_home))
    def _():
        arrived(gtile, G_AT)

    abuf[me] = gtile[...]
    bbuf[r, mine] = gtile[...]
    for at, steps, name in (("z", 2, "m2"), ("z", -2, "p2"), ("z", 1, "m1"), ("z", -1, "p1"), ("y", 0, "y0")):
        b_send(at, steps, name, r)
    for j, dy in enumerate((1, 3, 2)):
        copy(abuf.at[me], abuf.at[me], A_AT + j, A_AT + me, (r, at_col(0, dy))).start()
    a_spread(me, 3)
    b_share(r)
    b_pass("m1", "p1", "m2", "p2")
    a_pass(1, 1)
    a_pass(2, 3)
    a_pass(3, 2)
    x_pass("y3", "n2")
    b_pass("m3", "p3", "q4", "y0", "n1", "y1", "n2", "y2", "n3", "y3", "r4")
    for dx in (1, 3, 2):
        for dy in range(YH):
            s = beside(dx, dy)
            arrived(abuf.at[s], A_AT + s)

    squared = jnp.zeros((half, rows), jnp.float32)
    for s in range(N_ROW):
        arrived(bbuf.at[s, other], BC_AT + s)
        squared = squared + jnp.dot(abuf[s], bbuf[s], preferred_element_type=jnp.float32)
    fbuf[me, mine] = (coef_b * gtile[...].astype(jnp.float32) + coef_c * squared).astype(jnp.bfloat16)

    def f_share(s):
        copy(fbuf.at[s, mine], fbuf.at[s, mine], FC_AT + s, FC_AT + s, sibling).start()

    def f_spread(s, first):
        for i, dx in enumerate((1, 3, 2)):
            copy(
                fbuf.at[s, mine], fbuf.at[s, mine], F_AT + first + i, F_AT + s, (r, at_col(dx, 0))
            ).start()

    def f_apply(dx):
        for dy in range(YH):
            s = beside(dx, dy)
            arrived(fbuf.at[s, other], FC_AT + s)
            acc[:, pl.ds(0, MAIN)] += jnp.dot(fbuf[s], xmain[s], preferred_element_type=jnp.float32)
            acc[:, pl.ds(MAIN, side)] += jnp.dot(fbuf[s], xtail[s], preferred_element_type=jnp.float32)

    for j, dy in enumerate((1, 3, 2)):
        copy(fbuf.at[me, mine], fbuf.at[me, mine], F_AT + j, F_AT + me, (r, at_col(0, dy))).start()
    f_spread(me, 3)
    f_share(me)
    acc[...] = coef_a * xown[...].astype(jnp.float32)
    for name in ("m3", "q4", "n3", "r4"):
        for part in BOTH:
            x_wait(name, part)
    unpack("m3", "p3", "q4", "y3", "n1", "n2", "n3", "r4")
    for j, dy in enumerate((1, 3, 2)):
        s = beside(0, YH - dy)
        arrived(fbuf.at[s, mine], F_AT + s)
        f_share(s)
        f_spread(s, 6 + 3 * j)
    done = 0
    for dx in (1, 3, 2):
        for dy in range(YH):
            s = beside(dx, dy)
            arrived(fbuf.at[s, mine], F_AT + s)
            f_share(s)
        f_apply(done)
        done = dx
    f_apply(done)
    o_ref[...] = (scale * acc[...]).astype(o_ref.dtype)

    for name in KIND:
        for part in BOTH:
            for piece, number in x_pieces(name, 0, part):
                left(piece, number)
    for number in range(15):
        left(abuf.at[0], A_AT + number)
        left(abuf.at[0], B_AT + number)
        left(abuf.at[0], F_AT + number)
    for place in range(YH):

        @pl.when(yh != place)
        def _():
            left(ysend.at[place], Y_AT + place)

    @pl.when(jnp.logical_not(at_home))
    def _():
        left(gsend, G_AT)

    def all_left(s, carry):
        left(cbuf.at[s], CORE_AT + s)
        left(cbuf.at[s], BC_AT + s)
        left(cbuf.at[s], FC_AT + s)

        @pl.when(s // YH != x)
        def _():
            left(xsum.at[s], XR_AT + s)

        return carry

    lax.fori_loop(0, N_ROW, all_left, 0)


def solution(mesh):
    def step(iterate):
        rows, width = iterate.shape
        half, n = rows // 2, width * mesh.shape["col"]
        bf16 = jnp.bfloat16

        def body(*refs):
            kernel(math.sqrt(n), *refs)

        return pl.pallas_call(
            body,
            out_shape=jax.ShapeDtypeStruct((rows, width), bf16),
            in_specs=[pl.BlockSpec(memory_space=pl.ANY)],
            out_specs=pl.BlockSpec(memory_space=pltpu.VMEM),
            scratch_shapes=[
                pltpu.VMEM((rows, width), bf16),
                pltpu.VMEM((N_ROW, rows, MAIN), bf16),
                pltpu.VMEM((N_ROW, half, 2 * (width - MAIN)), bf16),
                pltpu.VMEM((N_ROW, rows, width - MAIN), bf16),
                pltpu.VMEM((N_ROW, rows, rows), bf16),
                pltpu.VMEM((N_ROW, half, rows), bf16),
                pltpu.VMEM((N_ROW, half, rows), bf16),
                pltpu.VMEM((X, YH, half, rows), bf16),
                pltpu.VMEM((YH, half, rows), bf16),
                pltpu.VMEM((YH, half, rows), bf16),
                pltpu.VMEM((half, rows), bf16),
                pltpu.VMEM((half, rows), bf16),
                pltpu.VMEM((N_ROW, half, rows), bf16),
                pltpu.VMEM((N_ROW, rows, rows), bf16),
                pltpu.VMEM((N_ROW, rows, rows), bf16),
                pltpu.VMEM((rows, width), jnp.float32),
                pltpu.SemaphoreType.DMA(()),
                pltpu.SemaphoreType.DMA((N_SEM,)),
                pltpu.SemaphoreType.DMA((N_SEM,)),
            ],
            compiler_params=pltpu.CompilerParams(
                collective_id=0, has_side_effects=True, vmem_limit_bytes=48 << 20
            ),
            cost_estimate=pl.CostEstimate(
                flops=2 * rows * N_ROW * rows * (2 * width + half), bytes_accessed=4 * rows * width, transcendentals=0
            ),
        )(iterate)

    return jax.shard_map(
        step, mesh=mesh, in_specs=(P("row", "col"),), out_specs=P("row", "col"), check_vma=False
    )
```

```python
import functools
import math

import jax
import jax.numpy as jnp
from jax import lax
from jax.experimental import pallas as pl
from jax.experimental.pallas import tpu as pltpu
from jax.sharding import PartitionSpec as P

MESH = pl.DeviceIdType.MESH
coef_a = 3.4445
coef_b = -4.775
coef_c = 2.0315

Z, X, YH = 8, 4, 4
N_ROW = 2 * Z

X_AT = 0
CORE_AT = X_AT + 45
XR_AT = CORE_AT + 16
Y_AT = XR_AT + 16
G_AT = Y_AT + 4
A_AT = G_AT + 1
B_AT = A_AT + 16
BC_AT = B_AT + 15
F_AT = BC_AT + 16
FC_AT = F_AT + 16
N_SEM = FC_AT + 16

HERE = (0, 0)
KIND = {
    "m1": (0, -1), "m2": (0, -2), "m3": (0, -3), "p1": (0, 1), "p2": (0, 2), "p3": (0, 3), "q4": (0, 4),
    "y0": (1, 0), "y1": (1, 1), "y2": (1, 2), "y3": (1, 3), "r4": (1, 4), "n1": (1, -1), "n2": (1, -2), "n3": (1, -3),
}
NUMBER = {name: i for i, name in enumerate(KIND)}
MAIN, CUT = 512, 128
BOTH = (0, 1)
ONWARD = {
    "m1": (("u", "m2", BOTH),), "m2": (("u", "m3", BOTH),),
    "p1": (("d", "p2", BOTH), ("y", "y1", BOTH)), "p2": (("d", "p3", BOTH), ("y", "y2", (0,))),
    "p3": (("d", "q4", BOTH), ("y", "y3", BOTH)),
    "y0": (("u", "n1", BOTH),), "y1": (("d", "y2", (1,)),), "y3": (("d", "r4", BOTH),),
    "n1": (("u", "n2", BOTH),), "n2": (("u", "n3", BOTH),),
}
PANEL = {
    "m1": (("y", 0, "n1"),), "p1": (("y", 0, "y1"),),
    "m2": (("z", 1, "m3"), ("y", 0, "n2")), "p2": (("z", -1, "p3"), ("z", -2, "q4"), ("y", 0, "y2")),
    "m3": (("y", 0, "n3"),), "p3": (("y", 0, "y3"),), "q4": (("y", 0, "r4"),),
}
T0, T1, T2 = (1, 0), (1, 1), (1, 2)
BLOCKS = (
    (HERE, HERE), ((0, -1), (0, 2)), ((0, 1), (0, -1)), (T1, (0, -1)),
    (HERE, (0, 1)), ((0, 2), (0, -1)), (T0, HERE), ((0, -2), T1),
    (HERE, (0, -1)), ((0, -2), (0, 2)), ((0, -1), T0), (T1, (0, -2)),
    ((0, -1), (0, 1)), ((0, -1), T1), ((0, 1), T0), ((0, -2), T2),
)
FIRST = (0, 2, 4, 6, 8, 10, 12, 14)
SECOND = (1, 3, 5, 7, 9, 11, 13)
LAST = (15,)


def pick(index, values):
    n = len(values)
    return sum(((n - lax.rem(index - i + n, n)) // n) * value for i, value in enumerate(values) if value)


def kernel(
    scale, x_ref, o_ref, xown, xmain, xpack, xtail, pbuf, cbuf, xsum, xrecv, ysend, yrecv, gsend, gtile, abuf, bbuf, fbuf, acc, fetch_sem, word_sem, send_sem, recv_sem
):
    rows, width = x_ref.shape
    half = rows // 2
    r, c = lax.axis_index("row"), lax.axis_index("col")
    yl, z = r // Z, lax.rem(r, Z)
    x, yh, k = c // (2 * YH), lax.rem(c // 2, YH), lax.rem(c, 2)
    me = yh * X + x
    mine = pl.ds(pl.multiple_of(k * half, half), half)
    other = pl.ds(pl.multiple_of((1 - k) * half, half), half)

    def at_row(side, steps):
        return lax.rem(yl + side, 2) * Z + lax.rem(z + steps + Z, Z)

    def at_col(dx, dy, dk=0):
        return lax.rem(x + dx, X) * (2 * YH) + lax.rem(yh + dy, YH) * 2 + lax.rem(k + dk, 2)

    link = {"u": (at_row(0, 1), c), "d": (at_row(0, -1), c), "y": (at_row(1, 0), c)}
    sibling = (r, at_col(0, 0, 1))

    def block_at(number):
        return at_row(pick(number, [a[0] for a, b in BLOCKS]), pick(number, [a[1] for a, b in BLOCKS])), at_row(
            pick(number, [b[0] for a, b in BLOCKS]), pick(number, [b[1] for a, b in BLOCKS])
        )

    def column(s):
        return lax.rem(s, X) * (2 * YH) + s // X * 2 + k

    to_row, to = block_at(x * YH + yh)
    owner = (to_row, column(to))
    at_home = jnp.logical_and(to_row == r, to == me)

    fetch = pltpu.make_async_copy(x_ref, xown, fetch_sem)
    fetch.start()
    barrier = pltpu.get_barrier_semaphore()
    outer = (at_row(1, 0), at_col(0, 2 * yl + YH - 1))
    partners = [*link.values(), sibling, outer, (r, at_col(1, 0)), (r, at_col(X - 1, 0))]
    for partner in partners:
        pl.semaphore_signal(barrier, inc=1, device_id=partner, device_id_type=MESH)

    pl.semaphore_wait(barrier, len(partners))

    def tell(number, *devices):
        for device in devices:
            pl.semaphore_signal(word_sem.at[number], inc=1, device_id=device, device_id_type=MESH)

    def hear(number, count):
        pl.semaphore_wait(word_sem.at[number], count)

    def copy(src, dst, sent, received, device):
        return pltpu.make_async_remote_copy(
            src_ref=src, dst_ref=dst, send_sem=send_sem.at[sent], recv_sem=recv_sem.at[received],
            device_id=device, device_id_type=MESH,
        )

    def arrived(dst, received):
        copy(dst, dst, received, received, sibling).wait_recv()

    def left(src, sent):
        copy(src, src, sent, sent, sibling).wait_send()

    side = width - MAIN

    def pack(s):
        xpack[s, :, pl.ds(0, side)] = xtail[s, pl.ds(0, half), :]
        xpack[s, :, pl.ds(side, side)] = xtail[s, pl.ds(half, half), :]

    def unpack(*names):
        for name in names:
            s = at_row(*KIND[name])
            xtail[s, pl.ds(0, half), :] = xpack[s, :, pl.ds(0, side)]
            xtail[s, pl.ds(half, half), :] = xpack[s, :, pl.ds(side, side)]

    def x_pieces(name, s, part):
        number = X_AT + 3 * NUMBER[name]
        if part == 0:
            return [(xmain.at[s, pl.ds(0, CUT)], number)]
        return [(xmain.at[s, pl.ds(CUT, rows - CUT)], number + 1), (xpack.at[s], number + 2)]

    def x_send(at, name, s, part):
        for piece, number in x_pieces(name, s, part):
            copy(piece, piece, number, number, link[at]).start()

    def x_wait(name, part):
        for piece, number in x_pieces(name, at_row(*KIND[name]), part):
            arrived(piece, number)

    def x_onward(name, part, *only):
        for at, new, parts in ONWARD[name]:
            if part in parts and (not only or new in only):
                x_send(at, new, at_row(*KIND[name]), part)

    def x_pass(*names):
        for part in BOTH:
            for name in names:
                x_wait(name, part)
                x_onward(name, part)

    fetch.wait()
    xmain[r] = xown[:, pl.ds(0, MAIN)]
    xtail[r] = xown[:, pl.ds(MAIN, side)]
    pack(r)
    for part in BOTH:
        for at, name in (("u", "m1"), ("d", "p1"), ("y", "y0")):
            x_send(at, name, r, part)
    tell(0, (r, at_col(1, 0)))
    tell(1, link["y"], outer)

    def gram(n):
        a, b = BLOCKS[n]
        a, b = at_row(*a), at_row(*b)
        across = (((1,), (1,)), ((), ()))
        product = lax.dot_general(xmain[a], xmain[b], across, preferred_element_type=jnp.float32)
        product = product + lax.dot_general(xtail[a], xtail[b], across, preferred_element_type=jnp.float32)
        pbuf[n] = product.astype(jnp.bfloat16)
        copy(pbuf.at[n, other], cbuf.at[n], CORE_AT + n, CORE_AT + n, sibling).start()

    def reduce_x(n):
        arrived(cbuf.at[n], CORE_AT + n)
        total = pbuf[n, mine].astype(jnp.float32) + cbuf[n].astype(jnp.float32)
        xsum[n] = total.astype(jnp.bfloat16)
        to, place = n // YH, n % YH
        apart = lax.rem(x - to + X, X)

        @pl.when(apart != 0)
        def _():
            copy(
                xsum.at[n], xrecv.at[apart, place], XR_AT + n, XR_AT + apart * YH + place,
                (r, to * (2 * YH) + yh * 2 + k),
            ).start()

    def grams_and_sums(numbers, before):
        pending = list(before)
        for n in numbers:
            gram(n)
            pending.append(n)
            if len(pending) > 3:
                reduce_x(pending.pop(0))
        for n in pending:
            reduce_x(n)

    def reduce_y(place):
        total = xsum[x * YH + place].astype(jnp.float32)
        for i in range(1, X):
            arrived(xrecv.at[i, place], XR_AT + i * YH + place)
            total = total + xrecv[i, place].astype(jnp.float32)
        ysend[place] = total.astype(jnp.bfloat16)
        apart = lax.rem(yh - place + YH, YH)

        @pl.when(apart != 0)
        def _():
            copy(
                ysend.at[place], yrecv.at[apart], Y_AT + place, Y_AT + apart,
                (r, x * (2 * YH) + place * 2 + k),
            ).start()

    def deliver():
        total = ysend[yh].astype(jnp.float32)
        for j in range(1, YH):
            arrived(yrecv.at[j], Y_AT + j)
            total = total + yrecv[j].astype(jnp.float32)
        gsend[...] = total.astype(jnp.bfloat16)

        @pl.when(jnp.logical_not(at_home))
        def _():
            copy(gsend, gtile, G_AT, G_AT, owner).start()

        @pl.when(at_home)
        def _():
            gtile[...] = gsend[...]

    gram(FIRST[0])
    hear(0, 1)
    hear(1, 2)
    tell(2, (r, at_col(0, 1)))
    for part in BOTH:
        for name in ("m1", "p1", "y0"):
            x_wait(name, part)
            if name != "y0":
                x_onward(name, part)
    unpack("m1", "p1", "y0")
    grams_and_sums(FIRST[1:], FIRST[:1])
    for part in BOTH:
        x_wait("m2", part)
        x_wait("p2", part)
        x_onward("p2", part, "y2")
        x_wait("y1", part)
        x_onward("y1", part)
    for part in BOTH:
        x_onward("m2", part)
        x_onward("y0", part)
    unpack("m2", "p2", "y1")
    grams_and_sums(SECOND, ())
    hear(2, 1)
    for place in (0, 2):
        reduce_y(place)
    for part in BOTH:
        x_wait("y2", part)
    unpack("y2")
    for n in LAST:
        gram(n)
    for part in BOTH:
        x_onward("p2", part, "p3")
    for n in LAST:
        reduce_x(n)

    @pl.when(lax.rem(yh, 2) == 0)
    def _():
        deliver()

    for place in (1, 3):
        reduce_y(place)

    def b_send(at, steps, name, s):
        number = B_AT + NUMBER[name]
        device = link["y"] if at == "y" else (at_row(0, steps), c)
        copy(bbuf.at[s, mine], bbuf.at[s, mine], number, number, device).start()

    def b_share(s):
        copy(bbuf.at[s, mine], bbuf.at[s, mine], BC_AT + s, BC_AT + s, sibling).start()

    def b_pass(*names):
        for name in names:
            s = at_row(*KIND[name])
            arrived(bbuf.at[s, mine], B_AT + NUMBER[name])
            b_share(s)
            for at, steps, new in PANEL.get(name, ()):
                b_send(at, steps, new, s)

    def beside(dx, dy):
        return lax.rem(yh + dy, YH) * X + lax.rem(x + dx, X)

    def a_spread(s, first):
        for i, dx in enumerate((1, 3, 2)):
            copy(abuf.at[s], abuf.at[s], A_AT + first + i, A_AT + s, (r, at_col(dx, 0))).start()

    def a_pass(number, dy):
        s = beside(0, YH - dy)
        arrived(abuf.at[s], A_AT + s)
        a_spread(s, 3 + 3 * number)

    x_pass("n1", "p3")

    @pl.when(lax.rem(yh, 2) == 1)
    def _():
        deliver()


    @pl.when(jnp.logical_not(at_home))
    def _():
        arrived(gtile, G_AT)

    abuf[me] = gtile[...]
    bbuf[r, mine] = gtile[...]
    for at, steps, name in (("z", 2, "m2"), ("z", -2, "p2"), ("z", 1, "m1"), ("z", -1, "p1"), ("y", 0, "y0")):
        b_send(at, steps, name, r)
    for j, dy in enumerate((1, 3, 2)):
        copy(abuf.at[me], abuf.at[me], A_AT + j, A_AT + me, (r, at_col(0, dy))).start()
    a_spread(me, 3)
    b_share(r)
    b_pass("m1", "p1", "m2", "p2")
    a_pass(1, 1)
    a_pass(2, 3)
    a_pass(3, 2)
    x_pass("y3", "n2")
    b_pass("m3", "p3", "q4", "y0", "n1", "y1", "n2", "y2", "n3", "y3", "r4")
    for dx in (1, 3, 2):
        for dy in range(YH):
            s = beside(dx, dy)
            arrived(abuf.at[s], A_AT + s)

    squared = jnp.zeros((half, rows), jnp.float32)
    for s in range(N_ROW):
        arrived(bbuf.at[s, other], BC_AT + s)
        squared = squared + jnp.dot(abuf[s], bbuf[s], preferred_element_type=jnp.float32)
    fbuf[me, mine] = (coef_b * gtile[...].astype(jnp.float32) + coef_c * squared).astype(jnp.bfloat16)

    def f_share(s):
        copy(fbuf.at[s, mine], fbuf.at[s, mine], FC_AT + s, FC_AT + s, sibling).start()

    def f_spread(s, first):
        for i, dx in enumerate((1, 3, 2)):
            copy(
                fbuf.at[s, mine], fbuf.at[s, mine], F_AT + first + i, F_AT + s, (r, at_col(dx, 0))
            ).start()

    def f_apply(dx):
        for dy in range(YH):
            s = beside(dx, dy)
            arrived(fbuf.at[s, other], FC_AT + s)
            acc[:, pl.ds(0, MAIN)] += jnp.dot(fbuf[s], xmain[s], preferred_element_type=jnp.float32)
            acc[:, pl.ds(MAIN, side)] += jnp.dot(fbuf[s], xtail[s], preferred_element_type=jnp.float32)

    def f_send(s, number, dx, dy):
        copy(fbuf.at[s, mine], fbuf.at[s, mine], F_AT + number, F_AT + s, (r, at_col(dx, dy))).start()

    def f_wait(s):
        arrived(fbuf.at[s, mine], F_AT + s)
        f_share(s)

    ahead, back = 1 + 2 * k, 3 - 2 * k

    for j, dy in enumerate((1, 3, 2)):
        f_send(me, j, 0, dy)
    f_send(me, 3, ahead, 0)
    f_send(me, 4, back, 0)
    f_share(me)
    acc[...] = coef_a * xown[...].astype(jnp.float32)
    f_wait(beside(back, 0))
    f_send(beside(back, 0), 5, ahead, 0)
    f_wait(beside(ahead, 0))
    for j, dy in enumerate((1, 3, 2)):
        s = beside(0, YH - dy)
        f_wait(s)
        f_send(s, 6 + 3 * j, ahead, 0)
        f_send(s, 7 + 3 * j, back, 0)
        if dy == 2:
            f_send(s, 8 + 3 * j, 2, 0)
    for j, dy in enumerate((1, 3)):
        s = beside(back, YH - dy)
        f_wait(s)
        f_send(s, 8 + 3 * j, ahead, 0)
        f_wait(beside(ahead, YH - dy))
    for name in ("m3", "q4", "n3", "r4"):
        for part in BOTH:
            x_wait(name, part)
    unpack("m3", "p3", "q4", "y3", "n1", "n2", "n3", "r4")
    f_apply(0)
    f_wait(beside(back, 2))
    f_wait(beside(ahead, 2))
    f_apply(1)
    for dy in (0, 1, 3, 2):
        f_wait(beside(2, dy))
    f_apply(3)
    f_apply(2)
    o_ref[...] = (scale * acc[...]).astype(o_ref.dtype)

    for name in KIND:
        for part in BOTH:
            for piece, number in x_pieces(name, 0, part):
                left(piece, number)
    for number in range(15):
        left(abuf.at[0], A_AT + number)
        left(abuf.at[0], B_AT + number)
        left(abuf.at[0], F_AT + number)
    for place in range(YH):

        @pl.when(yh != place)
        def _():
            left(ysend.at[place], Y_AT + place)

    @pl.when(jnp.logical_not(at_home))
    def _():
        left(gsend, G_AT)

    def all_left(s, carry):
        left(cbuf.at[s], CORE_AT + s)
        left(cbuf.at[s], BC_AT + s)
        left(cbuf.at[s], FC_AT + s)

        @pl.when(s // YH != x)
        def _():
            left(xsum.at[s], XR_AT + s)

        return carry

    lax.fori_loop(0, N_ROW, all_left, 0)


def solution(mesh):
    def step(iterate):
        rows, width = iterate.shape
        half, n = rows // 2, width * mesh.shape["col"]
        bf16 = jnp.bfloat16

        def body(*refs):
            kernel(math.sqrt(n), *refs)

        return pl.pallas_call(
            body,
            out_shape=jax.ShapeDtypeStruct((rows, width), bf16),
            in_specs=[pl.BlockSpec(memory_space=pl.ANY)],
            out_specs=pl.BlockSpec(memory_space=pltpu.VMEM),
            scratch_shapes=[
                pltpu.VMEM((rows, width), bf16),
                pltpu.VMEM((N_ROW, rows, MAIN), bf16),
                pltpu.VMEM((N_ROW, half, 2 * (width - MAIN)), bf16),
                pltpu.VMEM((N_ROW, rows, width - MAIN), bf16),
                pltpu.VMEM((N_ROW, rows, rows), bf16),
                pltpu.VMEM((N_ROW, half, rows), bf16),
                pltpu.VMEM((N_ROW, half, rows), bf16),
                pltpu.VMEM((X, YH, half, rows), bf16),
                pltpu.VMEM((YH, half, rows), bf16),
                pltpu.VMEM((YH, half, rows), bf16),
                pltpu.VMEM((half, rows), bf16),
                pltpu.VMEM((half, rows), bf16),
                pltpu.VMEM((N_ROW, half, rows), bf16),
                pltpu.VMEM((N_ROW, rows, rows), bf16),
                pltpu.VMEM((N_ROW, rows, rows), bf16),
                pltpu.VMEM((rows, width), jnp.float32),
                pltpu.SemaphoreType.DMA(()),
                pltpu.SemaphoreType.REGULAR((3,)),
                pltpu.SemaphoreType.DMA((N_SEM,)),
                pltpu.SemaphoreType.DMA((N_SEM,)),
            ],
            compiler_params=pltpu.CompilerParams(
                collective_id=0, has_side_effects=True, vmem_limit_bytes=48 << 20
            ),
            cost_estimate=pl.CostEstimate(
                flops=2 * rows * N_ROW * rows * (2 * width + half), bytes_accessed=4 * rows * width, transcendentals=0
            ),
        )(iterate)

    return jax.shard_map(
        step, mesh=mesh, in_specs=(P("row", "col"),), out_specs=P("row", "col"), check_vma=False
    )
```

```python
import functools
import math

import jax
import jax.numpy as jnp
from jax import lax
from jax.experimental import pallas as pl
from jax.experimental.pallas import tpu as pltpu
from jax.sharding import PartitionSpec as P

MESH = pl.DeviceIdType.MESH
coef_a = 3.4445
coef_b = -4.775
coef_c = 2.0315

Z, X, YH = 8, 4, 4
N_ROW = 2 * Z

X_AT = 0
CORE_AT = X_AT + 45
XR_AT = CORE_AT + 16
Y_AT = XR_AT + 16
G_AT = Y_AT + 4
A_AT = G_AT + 1
B_AT = A_AT + 16
BC_AT = B_AT + 15
F_AT = BC_AT + 16
FC_AT = F_AT + 16
N_SEM = FC_AT + 16

HERE = (0, 0)
KIND = {
    "m1": (0, -1), "m2": (0, -2), "m3": (0, -3), "p1": (0, 1), "p2": (0, 2), "p3": (0, 3), "q4": (0, 4),
    "y0": (1, 0), "y1": (1, 1), "y2": (1, 2), "y3": (1, 3), "r4": (1, 4), "n1": (1, -1), "n2": (1, -2), "n3": (1, -3),
}
NUMBER = {name: i for i, name in enumerate(KIND)}
MAIN, CUT = 512, 128
BOTH = (0, 1)
ONWARD = {
    "m1": (("u", "m2", BOTH),), "m2": (("u", "m3", BOTH),),
    "p1": (("d", "p2", BOTH), ("y", "y1", BOTH)), "p2": (("d", "p3", BOTH), ("y", "y2", (0,))),
    "p3": (("d", "q4", BOTH), ("y", "y3", BOTH)),
    "y0": (("u", "n1", BOTH),), "y1": (("d", "y2", (1,)),), "y3": (("d", "r4", BOTH),),
    "n1": (("u", "n2", BOTH),), "n2": (("u", "n3", BOTH),),
}
PANEL = {
    "m1": (("y", 0, "n1"),), "p1": (("y", 0, "y1"),),
    "m2": (("z", 1, "m3"), ("y", 0, "n2")), "p2": (("z", -1, "p3"), ("z", -2, "q4"), ("y", 0, "y2")),
    "m3": (("y", 0, "n3"),), "p3": (("y", 0, "y3"),), "q4": (("y", 0, "r4"),),
}
T0, T1, T2 = (1, 0), (1, 1), (1, 2)
BLOCKS = (
    (HERE, HERE), ((0, -1), (0, 2)), ((0, 1), (0, -1)), (T1, (0, -1)),
    (HERE, (0, 1)), ((0, 2), (0, -1)), (T0, HERE), ((0, -2), T1),
    (HERE, (0, -1)), ((0, -2), (0, 2)), ((0, -1), T0), (T1, (0, -2)),
    ((0, -1), (0, 1)), ((0, -1), T1), ((0, 1), T0), ((0, -2), T2),
)
FIRST = (0, 2, 4, 6, 8, 10, 12, 14)
SECOND = (1, 3, 5, 7, 9, 11, 13)
LAST = (15,)


def pick(index, values):
    n = len(values)
    return sum(((n - lax.rem(index - i + n, n)) // n) * value for i, value in enumerate(values) if value)


def kernel(
    scale, x_ref, o_ref, xown, xmain, xpack, xtail, pbuf, cbuf, xsum, xrecv, ysend, yrecv, gsend, gtile, abuf, bbuf, fbuf, acc, fetch_sem, word_sem, send_sem, recv_sem
):
    rows, width = x_ref.shape
    half = rows // 2
    r, c = lax.axis_index("row"), lax.axis_index("col")
    yl, z = r // Z, lax.rem(r, Z)
    x, yh, k = c // (2 * YH), lax.rem(c // 2, YH), lax.rem(c, 2)
    me = yh * X + x
    mine = pl.ds(pl.multiple_of(k * half, half), half)
    other = pl.ds(pl.multiple_of((1 - k) * half, half), half)

    def at_row(side, steps):
        return lax.rem(yl + side, 2) * Z + lax.rem(z + steps + Z, Z)

    def at_col(dx, dy, dk=0):
        return lax.rem(x + dx, X) * (2 * YH) + lax.rem(yh + dy, YH) * 2 + lax.rem(k + dk, 2)

    link = {"u": (at_row(0, 1), c), "d": (at_row(0, -1), c), "y": (at_row(1, 0), c)}
    sibling = (r, at_col(0, 0, 1))

    def block_at(number):
        return at_row(pick(number, [a[0] for a, b in BLOCKS]), pick(number, [a[1] for a, b in BLOCKS])), at_row(
            pick(number, [b[0] for a, b in BLOCKS]), pick(number, [b[1] for a, b in BLOCKS])
        )

    def column(s):
        return lax.rem(s, X) * (2 * YH) + s // X * 2 + k

    to_row, to = block_at(x * YH + yh)
    owner = (to_row, column(to))
    at_home = jnp.logical_and(to_row == r, to == me)

    fetch = pltpu.make_async_copy(x_ref, xown, fetch_sem)
    fetch.start()
    barrier = pltpu.get_barrier_semaphore()
    outer = (at_row(1, 0), at_col(0, 2 * yl + YH - 1))
    partners = [*link.values(), sibling, outer, (r, at_col(1, 0)), (r, at_col(X - 1, 0))]
    for partner in partners:
        pl.semaphore_signal(barrier, inc=1, device_id=partner, device_id_type=MESH)

    pl.semaphore_wait(barrier, len(partners))

    def tell(number, *devices):
        for device in devices:
            pl.semaphore_signal(word_sem.at[number], inc=1, device_id=device, device_id_type=MESH)

    def hear(number, count):
        pl.semaphore_wait(word_sem.at[number], count)

    def copy(src, dst, sent, received, device):
        return pltpu.make_async_remote_copy(
            src_ref=src, dst_ref=dst, send_sem=send_sem.at[sent], recv_sem=recv_sem.at[received],
            device_id=device, device_id_type=MESH,
        )

    def arrived(dst, received):
        copy(dst, dst, received, received, sibling).wait_recv()

    def left(src, sent):
        copy(src, src, sent, sent, sibling).wait_send()

    side = width - MAIN

    def pack(s):
        xpack[s, :, pl.ds(0, side)] = xtail[s, pl.ds(0, half), :]
        xpack[s, :, pl.ds(side, side)] = xtail[s, pl.ds(half, half), :]

    def unpack(*names):
        for name in names:
            s = at_row(*KIND[name])
            xtail[s, pl.ds(0, half), :] = xpack[s, :, pl.ds(0, side)]
            xtail[s, pl.ds(half, half), :] = xpack[s, :, pl.ds(side, side)]

    def x_pieces(name, s, part):
        number = X_AT + 3 * NUMBER[name]
        if part == 0:
            return [(xmain.at[s, pl.ds(0, CUT)], number)]
        return [(xmain.at[s, pl.ds(CUT, rows - CUT)], number + 1), (xpack.at[s], number + 2)]

    def x_send(at, name, s, part):
        for piece, number in x_pieces(name, s, part):
            copy(piece, piece, number, number, link[at]).start()

    def x_wait(name, part):
        for piece, number in x_pieces(name, at_row(*KIND[name]), part):
            arrived(piece, number)

    def x_onward(name, part, *only):
        for at, new, parts in ONWARD[name]:
            if part in parts and (not only or new in only):
                x_send(at, new, at_row(*KIND[name]), part)

    def x_pass(*names):
        for part in BOTH:
            for name in names:
                x_wait(name, part)
                x_onward(name, part)

    fetch.wait()
    xmain[r] = xown[:, pl.ds(0, MAIN)]
    xtail[r] = xown[:, pl.ds(MAIN, side)]
    pack(r)
    for part in BOTH:
        for at, name in (("u", "m1"), ("d", "p1"), ("y", "y0")):
            x_send(at, name, r, part)
    tell(0, (r, at_col(1, 0)))
    tell(1, link["y"], outer)

    def gram(n):
        a, b = BLOCKS[n]
        a, b = at_row(*a), at_row(*b)
        across = (((1,), (1,)), ((), ()))
        product = lax.dot_general(xmain[a], xmain[b], across, preferred_element_type=jnp.float32)
        product = product + lax.dot_general(xtail[a], xtail[b], across, preferred_element_type=jnp.float32)
        pbuf[n] = product.astype(jnp.bfloat16)
        copy(pbuf.at[n, other], cbuf.at[n], CORE_AT + n, CORE_AT + n, sibling).start()

    def reduce_x(n):
        arrived(cbuf.at[n], CORE_AT + n)
        total = pbuf[n, mine].astype(jnp.float32) + cbuf[n].astype(jnp.float32)
        xsum[n] = total.astype(jnp.bfloat16)
        to, place = n // YH, n % YH
        apart = lax.rem(x - to + X, X)

        @pl.when(apart != 0)
        def _():
            copy(
                xsum.at[n], xrecv.at[apart, place], XR_AT + n, XR_AT + apart * YH + place,
                (r, to * (2 * YH) + yh * 2 + k),
            ).start()

    def grams_and_sums(numbers, before):
        pending = list(before)
        for n in numbers:
            gram(n)
            pending.append(n)
            if len(pending) > 3:
                reduce_x(pending.pop(0))
        for n in pending:
            reduce_x(n)

    def reduce_y(place):
        total = xsum[x * YH + place].astype(jnp.float32)
        for i in range(1, X):
            arrived(xrecv.at[i, place], XR_AT + i * YH + place)
            total = total + xrecv[i, place].astype(jnp.float32)
        ysend[place] = total.astype(jnp.bfloat16)
        apart = lax.rem(yh - place + YH, YH)

        @pl.when(apart != 0)
        def _():
            copy(
                ysend.at[place], yrecv.at[apart], Y_AT + place, Y_AT + apart,
                (r, x * (2 * YH) + place * 2 + k),
            ).start()

    def deliver():
        total = ysend[yh].astype(jnp.float32)
        for j in range(1, YH):
            arrived(yrecv.at[j], Y_AT + j)
            total = total + yrecv[j].astype(jnp.float32)
        gsend[...] = total.astype(jnp.bfloat16)

        @pl.when(jnp.logical_not(at_home))
        def _():
            copy(gsend, gtile, G_AT, G_AT, owner).start()

        @pl.when(at_home)
        def _():
            gtile[...] = gsend[...]

    gram(FIRST[0])
    hear(0, 1)
    hear(1, 2)
    tell(2, (r, at_col(0, 1)))
    for part in BOTH:
        for name in ("m1", "p1", "y0"):
            x_wait(name, part)
            if name != "y0":
                x_onward(name, part)
    unpack("m1", "p1", "y0")
    grams_and_sums(FIRST[1:], FIRST[:1])
    for part in BOTH:
        x_wait("m2", part)
        x_wait("p2", part)
        x_onward("p2", part, "y2")
        x_wait("y1", part)
        x_onward("y1", part)
    for part in BOTH:
        x_onward("m2", part)
        x_onward("y0", part)
    unpack("m2", "p2", "y1")
    grams_and_sums(SECOND, ())
    hear(2, 1)
    for place in (0, 2):
        reduce_y(place)
    for part in BOTH:
        x_wait("y2", part)
    unpack("y2")
    for n in LAST:
        gram(n)
    for part in BOTH:
        x_onward("p2", part, "p3")
    for n in LAST:
        reduce_x(n)

    @pl.when(lax.rem(yh, 2) == 0)
    def _():
        deliver()

    for place in (1, 3):
        reduce_y(place)

    def b_send(at, steps, name, s):
        number = B_AT + NUMBER[name]
        device = link["y"] if at == "y" else (at_row(0, steps), c)
        copy(bbuf.at[s, mine], bbuf.at[s, mine], number, number, device).start()

    def b_share(s):
        copy(bbuf.at[s, mine], bbuf.at[s, mine], BC_AT + s, BC_AT + s, sibling).start()

    def b_pass(*names):
        for name in names:
            s = at_row(*KIND[name])
            arrived(bbuf.at[s, mine], B_AT + NUMBER[name])
            b_share(s)
            for at, steps, new in PANEL.get(name, ()):
                b_send(at, steps, new, s)

    def beside(dx, dy):
        return lax.rem(yh + dy, YH) * X + lax.rem(x + dx, X)

    def a_spread(s, first):
        for i, dx in enumerate((1, 3, 2)):
            copy(abuf.at[s], abuf.at[s], A_AT + first + i, A_AT + s, (r, at_col(dx, 0))).start()

    def a_pass(number, dy):
        s = beside(0, YH - dy)
        arrived(abuf.at[s], A_AT + s)
        a_spread(s, 3 + 3 * number)

    x_pass("n1", "p3")

    @pl.when(lax.rem(yh, 2) == 1)
    def _():
        deliver()


    @pl.when(jnp.logical_not(at_home))
    def _():
        arrived(gtile, G_AT)

    abuf[me] = gtile[...]
    bbuf[r, mine] = gtile[...]
    for at, steps, name in (("z", 2, "m2"), ("z", -2, "p2"), ("z", 1, "m1"), ("z", -1, "p1"), ("y", 0, "y0")):
        b_send(at, steps, name, r)
    for j, dy in enumerate((1, 3, 2)):
        copy(abuf.at[me], abuf.at[me], A_AT + j, A_AT + me, (r, at_col(0, dy))).start()
    a_spread(me, 3)
    b_share(r)
    b_pass("m1", "p1", "y0", "m2", "p2")
    a_pass(1, 1)
    a_pass(2, 3)
    a_pass(3, 2)
    x_pass("y3", "n2")
    b_pass("n1", "y1", "m3", "p3", "q4", "n2", "y2", "n3", "y3", "r4")
    for dx in (1, 3, 2):
        for dy in range(YH):
            s = beside(dx, dy)
            arrived(abuf.at[s], A_AT + s)

    squared = jnp.zeros((half, rows), jnp.float32)
    for s in range(N_ROW):
        arrived(bbuf.at[s, other], BC_AT + s)
        squared = squared + jnp.dot(abuf[s], bbuf[s], preferred_element_type=jnp.float32)
    fbuf[me, mine] = (coef_b * gtile[...].astype(jnp.float32) + coef_c * squared).astype(jnp.bfloat16)

    def f_share(s):
        copy(fbuf.at[s, mine], fbuf.at[s, mine], FC_AT + s, FC_AT + s, sibling).start()

    def f_spread(s, first):
        for i, dx in enumerate((1, 3, 2)):
            copy(
                fbuf.at[s, mine], fbuf.at[s, mine], F_AT + first + i, F_AT + s, (r, at_col(dx, 0))
            ).start()

    def f_apply(dx):
        for dy in range(YH):
            s = beside(dx, dy)
            arrived(fbuf.at[s, other], FC_AT + s)
            acc[:, pl.ds(0, MAIN)] += jnp.dot(fbuf[s], xmain[s], preferred_element_type=jnp.float32)
            acc[:, pl.ds(MAIN, side)] += jnp.dot(fbuf[s], xtail[s], preferred_element_type=jnp.float32)

    def f_send(s, number, dx, dy):
        copy(fbuf.at[s, mine], fbuf.at[s, mine], F_AT + number, F_AT + s, (r, at_col(dx, dy))).start()

    def f_wait(s):
        arrived(fbuf.at[s, mine], F_AT + s)
        f_share(s)

    ahead, back = 1 + 2 * k, 3 - 2 * k

    for j, dy in enumerate((1, 3, 2)):
        f_send(me, j, 0, dy)
    f_send(me, 3, ahead, 0)
    f_send(me, 4, back, 0)
    f_share(me)
    acc[...] = coef_a * xown[...].astype(jnp.float32)
    f_wait(beside(back, 0))
    f_send(beside(back, 0), 5, ahead, 0)
    f_wait(beside(ahead, 0))
    for j, dy in enumerate((1, 3, 2)):
        s = beside(0, YH - dy)
        f_wait(s)
        f_send(s, 6 + 3 * j, ahead, 0)
        f_send(s, 7 + 3 * j, back, 0)
        if dy == 2:
            f_send(s, 8 + 3 * j, 2, 0)
    for j, dy in enumerate((1, 3)):
        s = beside(back, YH - dy)
        f_wait(s)
        f_send(s, 8 + 3 * j, ahead, 0)
        f_wait(beside(ahead, YH - dy))
    for name in ("m3", "q4", "n3", "r4"):
        for part in BOTH:
            x_wait(name, part)
    unpack("m3", "p3", "q4", "y3", "n1", "n2", "n3", "r4")
    f_wait(beside(2, 0))
    f_apply(0)
    f_wait(beside(back, 2))
    f_wait(beside(ahead, 2))
    f_apply(1)
    f_wait(beside(2, YH - 1))
    f_apply(3)
    f_wait(beside(2, 1))
    f_wait(beside(2, 2))
    f_apply(2)
    o_ref[...] = (scale * acc[...]).astype(o_ref.dtype)

    for name in KIND:
        for part in BOTH:
            for piece, number in x_pieces(name, 0, part):
                left(piece, number)
    for number in range(15):
        left(abuf.at[0], A_AT + number)
        left(abuf.at[0], B_AT + number)
        left(abuf.at[0], F_AT + number)
    for place in range(YH):

        @pl.when(yh != place)
        def _():
            left(ysend.at[place], Y_AT + place)

    @pl.when(jnp.logical_not(at_home))
    def _():
        left(gsend, G_AT)

    def all_left(s, carry):
        left(cbuf.at[s], CORE_AT + s)
        left(cbuf.at[s], BC_AT + s)
        left(cbuf.at[s], FC_AT + s)

        @pl.when(s // YH != x)
        def _():
            left(xsum.at[s], XR_AT + s)

        return carry

    lax.fori_loop(0, N_ROW, all_left, 0)


def solution(mesh):
    def step(iterate):
        rows, width = iterate.shape
        half, n = rows // 2, width * mesh.shape["col"]
        bf16 = jnp.bfloat16

        def body(*refs):
            kernel(math.sqrt(n), *refs)

        return pl.pallas_call(
            body,
            out_shape=jax.ShapeDtypeStruct((rows, width), bf16),
            in_specs=[pl.BlockSpec(memory_space=pl.ANY)],
            out_specs=pl.BlockSpec(memory_space=pltpu.VMEM),
            scratch_shapes=[
                pltpu.VMEM((rows, width), bf16),
                pltpu.VMEM((N_ROW, rows, MAIN), bf16),
                pltpu.VMEM((N_ROW, half, 2 * (width - MAIN)), bf16),
                pltpu.VMEM((N_ROW, rows, width - MAIN), bf16),
                pltpu.VMEM((N_ROW, rows, rows), bf16),
                pltpu.VMEM((N_ROW, half, rows), bf16),
                pltpu.VMEM((N_ROW, half, rows), bf16),
                pltpu.VMEM((X, YH, half, rows), bf16),
                pltpu.VMEM((YH, half, rows), bf16),
                pltpu.VMEM((YH, half, rows), bf16),
                pltpu.VMEM((half, rows), bf16),
                pltpu.VMEM((half, rows), bf16),
                pltpu.VMEM((N_ROW, half, rows), bf16),
                pltpu.VMEM((N_ROW, rows, rows), bf16),
                pltpu.VMEM((N_ROW, rows, rows), bf16),
                pltpu.VMEM((rows, width), jnp.float32),
                pltpu.SemaphoreType.DMA(()),
                pltpu.SemaphoreType.REGULAR((3,)),
                pltpu.SemaphoreType.DMA((N_SEM,)),
                pltpu.SemaphoreType.DMA((N_SEM,)),
            ],
            compiler_params=pltpu.CompilerParams(
                collective_id=0, has_side_effects=True, vmem_limit_bytes=48 << 20
            ),
            cost_estimate=pl.CostEstimate(
                flops=2 * rows * N_ROW * rows * (2 * width + half), bytes_accessed=4 * rows * width, transcendentals=0
            ),
        )(iterate)

    return jax.shard_map(
        step, mesh=mesh, in_specs=(P("row", "col"),), out_specs=P("row", "col"), check_vma=False
    )
```
